512 devices in a mesh: rows: 32 (over z, y_hi, core), protos: 16 (over x, y_lo).
Axes of the slice: x: 4, y: 8 (y_hi: 2, y_lo: 4; y = y_hi * 4 + y_lo), z: 8, core: 2. Of those that a mesh axis runs over, the one named last changes fastest.
Arguments:
- student_patches: bfloat16 [2, 64, 256, 256], P(None, 'rows'), may hold values from -6 to 6
- teacher_patches: bfloat16 [2, 64, 256, 256], P(None, 'rows'), may hold values from -6 to 6
- positions: int32 [2, 64, 64], P(None, 'rows'), may hold values from 0 to 255, as said below
- prototypes: bfloat16 [256, 65536], P('rows', 'protos'), may hold values from -1 to 1
- loss_scale: float32 [1], replicated, may hold values from 327680 to 2621440
Outputs:
- grad_student: float32 [2, 4096, 256], P(None, 'rows', 'protos')
- grad_protos: float32 [256, 65536], P('rows', 'protos')
The draws below stay inside these ranges and needn't reach their ends.
Inputs may be any that keep to these rules, and one draw needn't show every extreme that they name: Each image's 64 positions are distinct and increasing.
All inputs are finite; a program needn't handle non-finite values.
Results may differ from the reference program's by a relative error of at most 0.027.
Values may be sent and summed in bfloat16 or wider, within the bound.
A program may use at most 64 MiB of HBM per device.

```python
import math
import jax
import jax.numpy as jnp
from jax import lax

K = 256
PATCHES = 256
MASKED = 64
IMG_DEV = 2
MICRO = 2
ITERS = 3
IMAGES = 64
ROWS_MB = 4096
PROTOS = 65536
N_ROWS = 32


def common_parts(key):
    count = max(8, min(64, PROTOS // 16))
    centers = jax.random.normal(jax.random.fold_in(key, 501), (K, count), jnp.float32)
    picks = jax.random.randint(jax.random.fold_in(key, 502), (MICRO, IMAGES, 3), 0, count)
    return (centers, picks)


def mixed_patches(centers, picks, weights, noise):
    chosen = jnp.transpose(centers)[picks]
    mixture = noise
    for member in range(3):
        mixture = mixture + weights[..., member:member + 1] * chosen[:, :, None, member, :]
    return jnp.clip(mixture, -6.0, 6.0)


def patch_draw_normal(key, centers, picks):
    weight_key, noise_key = jax.random.split(key, 2)
    weights = jax.random.uniform(weight_key, (MICRO, IMAGES, PATCHES, 3), jnp.float32, 0.2, 1.0)
    noise = 0.5 * jax.random.normal(noise_key, (MICRO, IMAGES, PATCHES, K), jnp.float32)
    return mixed_patches(centers, picks, weights, noise)


def draw_teacher_patches(key, part):
    centers, picks = common_parts(key)
    key = jax.random.fold_in(key, 21)
    values = patch_draw_normal(key, centers, picks)
    return values.astype(jnp.bfloat16)


def draw_student_patches(key, part):
    centers, picks = common_parts(key)
    key = jax.random.fold_in(key, 31)
    values = patch_draw_normal(key, centers, picks)
    return values.astype(jnp.bfloat16)


def draw_prototypes(key, part):
    centers, picks = common_parts(key)
    key = jax.random.fold_in(key, 41)
    owner_key, noise_key = jax.random.split(key, 2)
    owner = jax.random.randint(owner_key, (PROTOS,), 0, centers.shape[1])
    spread = 0.5
    noise = jax.random.normal(noise_key, (K, PROTOS), jnp.float32)
    values = (centers[:, owner] + spread * noise) * K ** (-0.5)
    return jnp.clip(values, -1.0, 1.0).astype(jnp.bfloat16)


def draw_positions(key, part):
    key = jax.random.fold_in(key, 7)
    keys = jax.random.split(key, MICRO * IMAGES)

    def one_image(image_key):
        return jnp.sort(jax.random.permutation(image_key, PATCHES)[:MASKED])
    picks = jax.vmap(one_image)(keys)
    return picks.reshape(MICRO, IMAGES, MASKED).astype(jnp.int32)


def setup_inputs(seed: int = 0) -> dict:
    arg_keys = jax.random.split(jax.random.key(seed), 6)
    return {
        "student_patches": draw_student_patches(jax.random.fold_in(arg_keys[5], 71), 0),
        "teacher_patches": draw_teacher_patches(jax.random.fold_in(arg_keys[5], 71), 0),
        "positions": draw_positions(jax.random.fold_in(arg_keys[5], 71), 0),
        "prototypes": draw_prototypes(jax.random.fold_in(arg_keys[5], 71), 0),
        "loss_scale": jnp.clip(jnp.exp(jax.random.uniform(arg_keys[4], (1,), jnp.float32, math.log(327680.0), math.log(2621440))), 327680.0, 2621440),
    }


teacher_temp = 0.07
student_temp = 0.1
epsilon = 1e-06

def pick_rows(patches, positions):
    picked = jnp.take_along_axis(patches, positions[..., None], axis=2)
    return picked.reshape(picked.shape[0], picked.shape[1] * picked.shape[2], picked.shape[3])

def unit_rows(values):
    widened = values.astype(jnp.float32)
    factor = lax.rsqrt(lax.optimization_barrier(jnp.sum(widened * widened, axis=-1, keepdims=True)) + epsilon)
    return (widened * factor, factor)

def reference(student_patches, teacher_patches, positions, prototypes, loss_scale):
    student_unit, student_factor = unit_rows(pick_rows(student_patches, positions))
    teacher_unit = unit_rows(pick_rows(teacher_patches, positions))[0]
    student_half = student_unit.astype(jnp.bfloat16)
    teacher_half = teacher_unit.astype(jnp.bfloat16)
    proto_wide = prototypes.astype(jnp.float32)
    proto_factor = lax.rsqrt(lax.optimization_barrier(jnp.sum(proto_wide * proto_wide, axis=0, keepdims=True)) + epsilon)
    proto_unit = proto_wide * proto_factor
    proto_float = proto_unit.astype(jnp.bfloat16).astype(jnp.float32)
    block_rows = IMG_DEV * MASKED

    def blocks_of(values):
        return values.reshape(MICRO, N_ROWS, block_rows, values.shape[-1]).transpose(1, 0, 2, 3)
    teacher_blocks = blocks_of(teacher_half)
    student_blocks = blocks_of(student_half)
    unit_blocks = blocks_of(student_unit)
    factor_blocks = blocks_of(student_factor)

    def kernel_of(teacher_block):
        scores = jnp.einsum('mrk,kp->mrp', teacher_block.astype(jnp.float32), proto_float)
        return jnp.exp(scores / teacher_temp)
    row_scale = jnp.ones((N_ROWS, MICRO, block_rows), jnp.float32)
    col_scale = jnp.ones((MICRO, PROTOS), jnp.float32)
    for sweep_step in range(ITERS):

        def add_columns(carry, pieces):
            teacher_block, row_block = pieces
            return (carry + lax.optimization_barrier(jnp.sum(row_block[:, :, None] * kernel_of(teacher_block), axis=1)), None)
        col_total, unused = lax.scan(add_columns, jnp.zeros((MICRO, PROTOS), jnp.float32), (teacher_blocks, row_scale))
        col_scale = 1.0 / col_total

        def new_rows(teacher_block):
            return 1.0 / lax.optimization_barrier(jnp.sum(kernel_of(teacher_block) * col_scale[:, None, :], axis=2))
        row_scale = lax.map(new_rows, teacher_blocks)
    row_count = MICRO * ROWS_MB
    factor_scale = loss_scale[0] / (row_count * student_temp)

    def finish(carry, pieces):
        teacher_block, student_block, unit_block, factor_block, row_block = pieces
        kernel = kernel_of(teacher_block)
        targets = row_block[:, :, None] * kernel * col_scale[:, None, :]
        logits = jnp.einsum('mrk,kp->mrp', student_block.astype(jnp.float32), proto_float) / student_temp
        exponent = jnp.exp(logits)
        totals = lax.optimization_barrier(jnp.sum(exponent, axis=2))
        slopes_half = ((exponent / totals[:, :, None] - targets) * factor_scale).astype(jnp.bfloat16)
        slopes = lax.optimization_barrier(slopes_half).astype(jnp.float32)
        feature_grad = jnp.einsum('mrp,kp->mrk', slopes, proto_float)
        inner_dot = lax.optimization_barrier(jnp.sum(unit_block * feature_grad, axis=2, keepdims=True))
        grad_block = (feature_grad - unit_block * inner_dot) * factor_block
        proto_sum = jnp.einsum('mrk,mrp->kp', student_block.astype(jnp.float32), slopes)
        column_dot = lax.optimization_barrier(jnp.sum(proto_unit * proto_sum, axis=0, keepdims=True))
        proto_term = (proto_sum - proto_unit * column_dot) * proto_factor
        rounded = lax.optimization_barrier(proto_term.astype(jnp.bfloat16)).astype(jnp.float32)
        return (carry + rounded, grad_block)
    start_carry = jnp.zeros((K, PROTOS), jnp.float32)
    grad_protos, grad_blocks = lax.scan(finish, start_carry, (teacher_blocks, student_blocks, unit_blocks, factor_blocks, row_scale))
    grad_student = grad_blocks.transpose(1, 0, 2, 3).reshape(MICRO, ROWS_MB, K)
    return (grad_student, grad_protos)
```

```python
import math

import jax
import jax.numpy as jnp
from jax import lax
from jax.experimental import pallas as pl
from jax.experimental.pallas import tpu as pltpu
from jax.sharding import PartitionSpec as P

ITERS = 3
LOG2E = 1.4426950408889634
TEACHER_EXP2 = LOG2E / 0.07
STUDENT_EXP2 = LOG2E / 0.1
EPSILON = 1e-6
MESH = pl.DeviceIdType.MESH
F32 = jnp.float32
BF16 = jnp.bfloat16


def dot(a, b, ca, cb):
    return lax.dot_general(a, b, (((ca,), (cb,)), ((), ())), preferred_element_type=F32)


def kernel(
    sp_hbm, tp_hbm, pos_ref, pr_ref, scale_ref,
    gs_ref, gp_ref,
    sp, tp, send_p, pg, pu, ph, pfac,
    tx, sx, th, sh, sht, ut, sfac,
    kmat, emat, slopes,
    colbuf, rowbuf1, rowbuf2, csc, rb, tb,
    send_r, rr, pterm, fs, fr, gsend, grecv,
    local_sem, pg_send, pg_recv,
    tx_send, tx_recv, sx_send, sx_recv,
    col_send, col_recv, row1_send, row1_recv, row2_send, row2_recv,
    rr_send, rr_recv, fr_send, fr_recv, gr_send, gr_recv,
):
    me = lax.axis_index("rows")
    mp = lax.axis_index("protos")
    z, h, c = me // 4, lax.rem(me // 2, 2), lax.rem(me, 2)
    x, l = mp // 4, lax.rem(mp, 4)
    q = h * 2 + c
    y = h * 4 + l

    def rows_dev(d):
        return (lax.rem(me + d, 32), mp)

    def z_dev(d):
        return (lax.rem(z + d, 8) * 4 + q, mp)

    def cx_dev(i):
        dx, dc = i // 2, lax.rem(i, 2)
        return (z * 4 + h * 2 + lax.rem(c + dc, 2), lax.rem(x + dx, 4) * 4 + l)

    def y_dev(d):
        other = lax.rem(y + d, 8)
        return (z * 4 + (other // 4) * 2 + c, x * 4 + lax.rem(other, 4))

    barrier = pltpu.get_barrier_semaphore()

    def greet(group, count):
        def body(d, carry):
            pl.semaphore_signal(barrier, inc=1, device_id=group(d), device_id_type=MESH)
            return carry
        lax.fori_loop(1, count, body, 0)

    greet(rows_dev, 32)
    greet(cx_dev, 8)
    greet(y_dev, 8)

    load_t = pltpu.make_async_copy(tp_hbm, tp, local_sem.at[0])
    load_t.start()
    load_s = pltpu.make_async_copy(sp_hbm, sp, local_sem.at[1])
    load_s.start()

    wide = pr_ref[...].astype(F32)
    for other in range(4):
        first = wide[:, other * 1024 : other * 1024 + 512]
        second = wide[:, other * 1024 + 512 : other * 1024 + 1024]
        send_p[other] = jnp.concatenate([first, second], axis=0).astype(BF16)
    pg[pl.ds(me, 1)] = send_p[pl.ds(q, 1)]

    pl.semaphore_wait(barrier, 45)

    def send_proto(d, carry):
        target = lax.rem(me + d, 32)
        pltpu.make_async_remote_copy(
            send_p.at[lax.rem(target, 4)], pg.at[me], pg_send.at[d], pg_recv.at[d],
            device_id=(target, mp), device_id_type=MESH,
        ).start()
        return carry

    lax.fori_loop(1, 32, send_proto, 0)

    def pick(patches, m):
        parts = []
        for image in range(2):
            where = jnp.broadcast_to(pos_ref[m, image : image + 1, :], (256, 64))
            hot = (lax.broadcasted_iota(jnp.int32, (256, 64), 0) == where).astype(F32).astype(BF16)
            parts.append(dot(hot, patches[m, image], 0, 0))
        return jnp.concatenate(parts, axis=0).astype(BF16)

    core_dev = (z * 4 + h * 2 + (1 - c), mp)
    y4_dev = (z * 4 + (1 - h) * 2 + c, mp)
    q_far = (1 - h) * 2 + c
    mine = pl.ds(pl.multiple_of(x * 32, 32), 32)

    def far_copy(buf, send, recv, i):
        return pltpu.make_async_remote_copy(
            buf.at[:, q_far, mine], buf.at[:, q_far, mine], send.at[i], recv.at[i],
            device_id=cx_dev(i), device_id_type=MESH,
        )

    def y4_copy(buf, send, recv):
        return pltpu.make_async_remote_copy(
            buf.at[:, q, mine], buf.at[:, q, mine], send.at[8], recv.at[8],
            device_id=y4_dev, device_id_type=MESH,
        )

    def core_copy(buf, send, recv):
        return pltpu.make_async_remote_copy(
            buf.at[:, q], buf.at[:, q], send.at[0], recv.at[0],
            device_id=core_dev, device_id_type=MESH,
        )

    load_t.wait()
    for m in range(2):
        tx[m, pl.ds(q, 1)] = pick(tp, m)[None]
    y4_copy(tx, tx_send, tx_recv).start()
    core_copy(tx, tx_send, tx_recv).start()
    load_s.wait()
    for m in range(2):
        sx[m, pl.ds(q, 1)] = pick(sp, m)[None]
    y4_copy(sx, sx_send, sx_recv).start()
    core_copy(sx, sx_send, sx_recv).start()

    def forward_far(buf, send, recv):
        y4_copy(buf, send, recv).wait_recv()

        def body(i, carry):
            far_copy(buf, send, recv, i).start()
            return carry

        lax.fori_loop(1, 8, body, 0)

    def rows_arrive(buf, send, recv):
        core_copy(buf, send, recv).wait_recv()

        def body(i, carry):
            far_copy(buf, send, recv, i).wait_recv()
            return carry

        lax.fori_loop(1, 8, body, 0)

    def rows_sent(buf, send, recv):
        y4_copy(buf, send, recv).wait_send()
        core_copy(buf, send, recv).wait_send()

        def body(i, carry):
            far_copy(buf, send, recv, i).wait_send()
            return carry

        lax.fori_loop(1, 8, body, 0)

    forward_far(tx, tx_send, tx_recv)
    forward_far(sx, sx_send, sx_recv)

    rows_arrive(tx, tx_send, tx_recv)
    for m in range(2):
        for part in range(4):
            values = tx[m, part].astype(F32)
            factor = lax.rsqrt(jnp.sum(values * values, axis=1, keepdims=True) + EPSILON)
            th[m, part * 128 : part * 128 + 128, :] = (values * factor).astype(BF16)

    rows_arrive(sx, sx_send, sx_recv)
    for m in range(2):
        for part in range(4):
            values = sx[m, part].astype(F32)
            turned = jnp.concatenate([values[:, :128].T, values[:, 128:].T], axis=0)
            factor = lax.rsqrt(jnp.sum(turned * turned, axis=0, keepdims=True) + EPSILON)
            unit = turned * factor
            at = slice(part * 128, part * 128 + 128)
            ut[m, :, at] = unit
            sht[m, :, at] = unit.astype(BF16)
            sfac[m, part] = jnp.broadcast_to(factor, (8, 128))
            sh[m, at, :] = jnp.concatenate([unit[:128, :].T, unit[128:, :].T], axis=1).astype(BF16)

    def wait_proto(d, carry):
        pltpu.make_async_remote_copy(
            send_p.at[0], pg.at[me], pg_send.at[d], pg_recv.at[d],
            device_id=rows_dev(d), device_id_type=MESH,
        ).wait_recv()
        return carry

    lax.fori_loop(1, 32, wait_proto, 0)

    def unpack(b, total):
        block = pg[b].astype(F32)
        rows = jnp.concatenate([block[0:8, :], block[8:16, :]], axis=1)
        pu[pl.ds(pl.multiple_of(b * 8, 8), 8), :] = rows
        return total + rows * rows

    total = lax.fori_loop(0, 32, unpack, jnp.zeros((8, 1024), F32))
    pfac[...] = jnp.broadcast_to(
        lax.rsqrt(jnp.sum(total, axis=0, keepdims=True) + EPSILON), (8, 1024)
    )

    def normalize(b, carry):
        at = pl.ds(pl.multiple_of(b * 16, 16), 16)
        unit = pu[at, :] * pfac[0:1, :]
        pu[at, :] = unit
        ph[at, :] = unit.astype(BF16)
        return carry

    lax.fori_loop(0, 16, normalize, 0)

    def tile_send(buf, send, recv, group):
        def body(d, carry):
            pltpu.make_async_remote_copy(
                buf.at[0], buf.at[d], send.at[d], recv.at[d], device_id=group(d), device_id_type=MESH
            ).start()
            return carry
        lax.fori_loop(1, 8, body, 0)

    def tile_recv(buf, send, recv, group):
        def body(d, carry):
            pltpu.make_async_remote_copy(
                buf.at[0], buf.at[d], send.at[d], recv.at[d], device_id=group(d), device_id_type=MESH
            ).wait_recv()
            return carry
        lax.fori_loop(1, 8, body, 0)
        return jnp.sum(buf[...], axis=0)

    def col_store(it, m, tile, sums):
        width = sums.shape[1] // 128
        for part in range(width):
            row = tile * width + part
            colbuf[it, m, 0, row : row + 1, :] = sums[:, part * 128 : part * 128 + 128]

    def lane_sums(block):
        return jnp.sum(block.T, axis=0, keepdims=True)

    def spread(row):
        return jnp.broadcast_to(row, (128, 128)).T

    def col_send_start(it, m):
        tile_send(colbuf.at[it, m], col_send.at[it, m], col_recv.at[it, m], z_dev)

    for m in range(2):
        for tile in range(4):
            at = slice(tile * 256, tile * 256 + 256)
            scores = dot(th[m], ph[:, at], 1, 0)
            values = jnp.exp2(scores * TEACHER_EXP2)
            kmat[m, :, at] = values
            col_store(0, m, tile, jnp.sum(values, axis=0, keepdims=True))
        col_send_start(0, m)

    for m in range(2):
        acc = None
        for tile in range(4):
            at = slice(tile * 256, tile * 256 + 256)
            logits = dot(sh[m], ph[:, at], 1, 0)
            values = jnp.exp2(logits * STUDENT_EXP2)
            emat[m, :, at] = values
            half = values[:, :128] + values[:, 128:]
            acc = half if acc is None else acc + half
        for part in range(4):
            rowbuf1[0, m, 0, 4 + part : 5 + part, :] = lane_sums(acc[part * 128 : part * 128 + 128, :])

    loss_factor = scale_ref[0] * (1.0 / (2 * 4096 * 0.1))

    for it in range(ITERS):
        for m in range(2):
            total = tile_recv(colbuf.at[it, m], col_send.at[it, m], col_recv.at[it, m], z_dev)
            csc[m] = 1.0 / total
            for part in range(4):
                at = slice(part * 128, part * 128 + 128)
                acc = jnp.zeros((128, 128), F32)
                for tile in range(8):
                    acc = acc + kmat[m, at, tile * 128 : tile * 128 + 128] * csc[m, tile : tile + 1, :]
                rowbuf1[it, m, 0, part : part + 1, :] = lane_sums(acc)
            if it > 0:
                rowbuf1[it, m, 0, 4:8, :] = jnp.zeros((4, 128), F32)
            tile_send(rowbuf1.at[it, m], row1_send.at[it, m], row1_recv.at[it, m], cx_dev)
        for m in range(2):
            total = tile_recv(rowbuf1.at[it, m], row1_send.at[it, m], row1_recv.at[it, m], cx_dev)
            rowbuf2[it, m, 0] = total
            tile_send(rowbuf2.at[it, m], row2_send.at[it, m], row2_recv.at[it, m], y_dev)
        for m in range(2):
            total = tile_recv(rowbuf2.at[it, m], row2_send.at[it, m], row2_recv.at[it, m], y_dev)
            inverse = 1.0 / total[0:4, :]
            if it == ITERS - 1:
                inverse = inverse * loss_factor
            for part in range(4):
                rb[m, part * 128 : part * 128 + 128, :] = spread(inverse[part : part + 1, :])
            if it == 0:
                denominator = loss_factor / total[4:8, :]
                for part in range(4):
                    tb[m, part * 128 : part * 128 + 128, :] = spread(denominator[part : part + 1, :])
            if it < ITERS - 1:
                for tile in range(8):
                    at = slice(tile * 128, tile * 128 + 128)
                    sums = jnp.sum(kmat[m, :, at] * rb[m], axis=0, keepdims=True)
                    col_store(it + 1, m, tile, sums)
                col_send_start(it + 1, m)

    for m in range(2):
        for tile in range(8):
            at = slice(tile * 128, tile * 128 + 128)
            target = kmat[m, :, at] * rb[m] * csc[m, tile : tile + 1, :]
            slopes[m, :, at] = (emat[m, :, at] * tb[m] - target).astype(BF16)

    for tile in range(4):
        at = slice(tile * 256, tile * 256 + 256)
        proto_sum = dot(sht[0], slopes[0, :, at], 1, 0) + dot(sht[1], slopes[1, :, at], 1, 0)
        unit = pu[:, at]
        column_dot = jnp.sum(unit * proto_sum, axis=0, keepdims=True)
        pterm[:, at] = (proto_sum - unit * column_dot) * pfac[0:1, at]

    def send_back(d, carry):
        target = lax.rem(me + d, 32)
        rows = pterm[pl.ds(pl.multiple_of(target * 8, 8), 8), :]
        packed = jnp.concatenate([rows[:, :512], rows[:, 512:]], axis=0)
        send_r[pl.ds(d, 1)] = packed.astype(BF16)[None]
        pltpu.make_async_remote_copy(
            send_r.at[d], rr.at[me], rr_send.at[d], rr_recv.at[d],
            device_id=(target, mp), device_id_type=MESH,
        ).start()
        return carry

    lax.fori_loop(1, 32, send_back, 0)
    own = pterm[pl.ds(pl.multiple_of(me * 8, 8), 8), :]
    rr[pl.ds(me, 1)] = jnp.concatenate([own[:, :512], own[:, 512:]], axis=0).astype(BF16)[None]

    for m in range(2):
        grad = dot(ph[...], slopes[m], 1, 1)
        unit = ut[m]
        inner = jnp.sum(unit * grad, axis=0, keepdims=True)
        grad = (grad - unit * inner).astype(BF16)
        for xx in range(4):
            for part in range(4):
                lane = ((part // 2) * 2 + m) * 128
                fs[xx * 2 + part % 2, :, lane : lane + 128] = grad[
                    xx * 64 : xx * 64 + 64, part * 128 : part * 128 + 128
                ]

    def fs_copy(i):
        slot = lax.rem(x + i // 2, 4) * 2 + lax.rem(c + lax.rem(i, 2), 2)
        return pltpu.make_async_remote_copy(
            fs.at[slot], fr.at[i], fr_send.at[i], fr_recv.at[i],
            device_id=cx_dev(i), device_id_type=MESH,
        )

    def fs_start(i, carry):
        fs_copy(i).start()
        return carry

    def fs_wait(i, carry):
        fs_copy(i).wait_recv()
        return carry

    lax.fori_loop(1, 8, fs_start, 0)
    fr[pl.ds(0, 1)] = fs[pl.ds(x * 2 + c, 1)]
    lax.fori_loop(1, 8, fs_wait, 0)

    def fs_sum(l_to, carry):
        at = pl.ds(pl.multiple_of(l_to * 16, 16), 16)
        total = fr[0, at, :].astype(F32)
        for slot in range(1, 8):
            total = total + fr[slot, at, :].astype(F32)
        total = total.astype(BF16)
        gsend[pl.ds(l_to, 1)] = total[:, :256][None]
        gsend[pl.ds(4 + l_to, 1)] = total[:, 256:][None]
        return carry

    lax.fori_loop(0, 4, fs_sum, 0)

    def gr_copy(d):
        return pltpu.make_async_remote_copy(
            gsend.at[lax.rem(y + d, 8)], grecv.at[d], gr_send.at[d], gr_recv.at[d],
            device_id=y_dev(d), device_id_type=MESH,
        )

    def gr_start(d, carry):
        gr_copy(d).start()
        return carry

    def gr_wait(d, carry):
        gr_copy(d).wait_recv()
        return carry

    lax.fori_loop(1, 8, gr_start, 0)
    grecv[pl.ds(0, 1)] = gsend[pl.ds(y, 1)]
    lax.fori_loop(1, 8, gr_wait, 0)
    total = jnp.sum(grecv[...].astype(F32), axis=0)
    for m in range(2):
        gs_ref[:, m * 128 : m * 128 + 128] = (
            total[:, m * 128 : m * 128 + 128] * sfac[m, pl.ds(q, 1)][0, 0:1, :]
        )

    def rr_copy(d):
        return pltpu.make_async_remote_copy(
            send_r.at[d], rr.at[me], rr_send.at[d], rr_recv.at[d],
            device_id=rows_dev(d), device_id_type=MESH,
        )

    def rr_wait(d, carry):
        rr_copy(d).wait_recv()
        return carry

    lax.fori_loop(1, 32, rr_wait, 0)
    for part in range(4):
        total = rr[part].astype(F32)
        for zz in range(1, 8):
            total = total + rr[zz * 4 + part].astype(F32)
        gp_ref[:, part * 1024 : part * 1024 + 512] = total[0:8, :]
        gp_ref[:, part * 1024 + 512 : part * 1024 + 1024] = total[8:16, :]

    rows_sent(tx, tx_send, tx_recv)
    rows_sent(sx, sx_send, sx_recv)

    def drain31(d, carry):
        pltpu.make_async_remote_copy(
            send_p.at[0], pg.at[me], pg_send.at[d], pg_recv.at[d],
            device_id=rows_dev(d), device_id_type=MESH,
        ).wait_send()
        rr_copy(d).wait_send()
        return carry

    lax.fori_loop(1, 32, drain31, 0)

    def drain7(d, carry):
        fs_copy(d).wait_send()
        gr_copy(d).wait_send()
        for it in range(ITERS):
            for m in range(2):
                for buf, send, recv, group in (
                    (colbuf, col_send, col_recv, z_dev),
                    (rowbuf1, row1_send, row1_recv, cx_dev),
                    (rowbuf2, row2_send, row2_recv, y_dev),
                ):
                    pltpu.make_async_remote_copy(
                        buf.at[it, m, 0], buf.at[it, m, d], send.at[it, m, d], recv.at[it, m, d],
                        device_id=group(d), device_id_type=MESH,
                    ).wait_send()
        return carry

    lax.fori_loop(1, 8, drain7, 0)


def local(student_patches, teacher_patches, positions, prototypes, loss_scale):
    vmem = pl.BlockSpec(memory_space=pltpu.VMEM)
    dma = pltpu.SemaphoreType.DMA
    grad_t, grad_protos = pl.pallas_call(
        kernel,
        out_shape=(
            jax.ShapeDtypeStruct((16, 256), F32),
            jax.ShapeDtypeStruct((8, 4096), F32),
        ),
        in_specs=[
            pl.BlockSpec(memory_space=pl.ANY),
            pl.BlockSpec(memory_space=pl.ANY),
            vmem,
            vmem,
            pl.BlockSpec(memory_space=pltpu.SMEM),
        ],
        out_specs=(vmem, vmem),
        scratch_shapes=[
            pltpu.VMEM((2, 2, 256, 256), BF16),
            pltpu.VMEM((2, 2, 256, 256), BF16),
            pltpu.VMEM((4, 16, 512), BF16),
            pltpu.VMEM((32, 16, 512), BF16),
            pltpu.VMEM((256, 1024), F32),
            pltpu.VMEM((256, 1024), BF16),
            pltpu.VMEM((8, 1024), F32),
            pltpu.VMEM((2, 4, 128, 256), BF16),
            pltpu.VMEM((2, 4, 128, 256), BF16),
            pltpu.VMEM((2, 512, 256), BF16),
            pltpu.VMEM((2, 512, 256), BF16),
            pltpu.VMEM((2, 256, 512), BF16),
            pltpu.VMEM((2, 256, 512), F32),
            pltpu.VMEM((2, 4, 8, 128), F32),
            pltpu.VMEM((2, 512, 1024), F32),
            pltpu.VMEM((2, 512, 1024), F32),
            pltpu.VMEM((2, 512, 1024), BF16),
            pltpu.VMEM((ITERS, 2, 8, 8, 128), F32),
            pltpu.VMEM((ITERS, 2, 8, 8, 128), F32),
            pltpu.VMEM((ITERS, 2, 8, 8, 128), F32),
            pltpu.VMEM((2, 8, 128), F32),
            pltpu.VMEM((2, 512, 128), F32),
            pltpu.VMEM((2, 512, 128), F32),
            pltpu.VMEM((32, 16, 512), BF16),
            pltpu.VMEM((32, 16, 512), BF16),
            pltpu.VMEM((256, 1024), F32),
            pltpu.VMEM((8, 64, 512), BF16),
            pltpu.VMEM((8, 64, 512), BF16),
            pltpu.VMEM((8, 16, 256), BF16),
            pltpu.VMEM((8, 16, 256), BF16),
            dma((2,)),
            dma((32,)),
            dma((32,)),
            dma((9,)),
            dma((9,)),
            dma((9,)),
            dma((9,)),
            dma((ITERS, 2, 8)),
            dma((ITERS, 2, 8)),
            dma((ITERS, 2, 8)),
            dma((ITERS, 2, 8)),
            dma((ITERS, 2, 8)),
            dma((ITERS, 2, 8)),
            dma((32,)),
            dma((32,)),
            dma((8,)),
            dma((8,)),
            dma((8,)),
            dma((8,)),
        ],
        compiler_params=pltpu.CompilerParams(
            collective_id=0, has_side_effects=True, vmem_limit_bytes=48 * 2**20
        ),
        cost_estimate=pl.CostEstimate(
            flops=2_200_000_000, bytes_accessed=2_000_000, transcendentals=2_000_000
        ),
        name="ibot_head",
    )(student_patches, teacher_patches, positions, prototypes, loss_scale)
    grad_student = jnp.transpose(grad_t.reshape(16, 2, 128), (1, 2, 0))
    return grad_student, grad_protos


def solution(mesh):
    in_specs = (
        P(None, "rows", None, None),
        P(None, "rows", None, None),
        P(None, "rows", None),
        P("rows", "protos"),
        P(),
    )
    out_specs = (P(None, "rows", "protos"), P("rows", "protos"))
    return jax.shard_map(local, mesh=mesh, in_specs=in_specs, out_specs=out_specs, check_vma=False)
```

```python
import math

import jax
import jax.numpy as jnp
from jax import lax
from jax.experimental import pallas as pl
from jax.experimental.pallas import tpu as pltpu
from jax.sharding import PartitionSpec as P

ITERS = 3
LOG2E = 1.4426950408889634
TEACHER_EXP2 = LOG2E / 0.07
STUDENT_EXP2 = LOG2E / 0.1
EPSILON = 1e-6
MESH = pl.DeviceIdType.MESH
F32 = jnp.float32
BF16 = jnp.bfloat16


def dot(a, b, ca, cb):
    return lax.dot_general(a, b, (((ca,), (cb,)), ((), ())), preferred_element_type=F32)


def kernel(
    sp_hbm, tp_hbm, pos_hbm, pr_hbm, scale_hbm,
    gs_ref, gp_ref,
    sp, tp, pos_ref, pr_ref, scale_ref, send_p, pg, pu, ph, pfac,
    tx, sx, th, sh, sht, ut, sfac,
    kmat, emat, slopes,
    colbuf, rowbuf1, rowbuf2, csc, rb, tb,
    send_r, rr, pterm, fs, fr, gsend, grecv,
    local_sem, pg_send, pg_recv,
    tx_send, tx_recv, sx_send, sx_recv,
    col_send, col_recv, row1_send, row1_recv, row2_send, row2_recv,
    rr_send, rr_recv, fr_send, fr_recv, gr_send, gr_recv,
):
    me = lax.axis_index("rows")
    mp = lax.axis_index("protos")
    z, h, c = me // 4, lax.rem(me // 2, 2), lax.rem(me, 2)
    x, l = mp // 4, lax.rem(mp, 4)
    q = h * 2 + c
    y = h * 4 + l

    drains = []

    def drain(first, count, copy):
        def wait(i, carry):
            copy(i).wait_send()
            return carry
        drains.append((first, count, wait))

    def flush():
        for first, count, wait in drains:
            lax.fori_loop(first, count, wait, 0)
        drains.clear()

    def z_dev(d):
        return (lax.rem(z + d, 8) * 4 + q, mp)

    def cx_dev(i):
        dx, dc = i // 2, lax.rem(i, 2)
        return (z * 4 + h * 2 + lax.rem(c + dc, 2), lax.rem(x + dx, 4) * 4 + l)

    def y_dev(d):
        other = lax.rem(y + d, 8)
        return (z * 4 + (other // 4) * 2 + c, x * 4 + lax.rem(other, 4))

    core_dev = (z * 4 + h * 2 + (1 - c), mp)
    y4_dev = (z * 4 + (1 - h) * 2 + c, mp)
    diag_dev = (z * 4 + (1 - h) * 2 + (1 - c), mp)

    barrier = pltpu.get_barrier_semaphore()
    pl.semaphore_signal(barrier, inc=1, device_id=diag_dev, device_id_type=MESH)

    def greet(d, carry):
        for group in (z_dev, y_dev, cx_dev):
            pl.semaphore_signal(barrier, inc=1, device_id=group(d), device_id_type=MESH)
        return carry

    lax.fori_loop(1, 8, greet, 0)

    load_p = pltpu.make_async_copy(pr_hbm, pr_ref, local_sem.at[2])
    load_p.start()
    load_pos = pltpu.make_async_copy(pos_hbm, pos_ref, local_sem.at[3])
    load_pos.start()
    load_scale = pltpu.make_async_copy(scale_hbm, scale_ref, local_sem.at[4])
    load_scale.start()
    load_t = pltpu.make_async_copy(tp_hbm, tp, local_sem.at[0])
    load_t.start()
    load_s = pltpu.make_async_copy(sp_hbm, sp, local_sem.at[1])
    load_s.start()

    load_p.wait()
    wide = pr_ref[...].astype(F32)
    for other in range(4):
        first = wide[:, other * 1024 : other * 1024 + 512]
        second = wide[:, other * 1024 + 512 : other * 1024 + 1024]
        send_p[other] = jnp.concatenate([first, second], axis=0).astype(BF16)
    pg[pl.ds(me, 1)] = send_p[pl.ds(q, 1)]

    pl.semaphore_wait(barrier, 22)

    def relative(j):
        return (h + (j // 2)) % 2 * 2 + (c + j % 2) % 2

    def quad_copy(j, target):
        return pltpu.make_async_remote_copy(
            send_p.at[relative(j)], pg.at[me], pg_send.at[j], pg_recv.at[j],
            device_id=target, device_id_type=MESH,
        )

    quad_copies = [quad_copy(2, y4_dev), quad_copy(3, diag_dev), quad_copy(1, core_dev)]

    def ring_copy(j, d):
        at = z * 4 + relative(j)
        return pltpu.make_async_remote_copy(
            pg.at[at], pg.at[at], pg_send.at[d * 4 + j], pg_recv.at[d * 4 + j],
            device_id=z_dev(d), device_id_type=MESH,
        )

    def ring_start(j):
        for d in (4, 5, 3, 6, 2, 7, 1):
            ring_copy(j, d).start()

    for copy in quad_copies:
        copy.start()
    ring_start(0)

    def pick(patches, m):
        parts = []
        for image in range(2):
            where = jnp.broadcast_to(pos_ref[m, image : image + 1, :], (256, 64))
            hot = (lax.broadcasted_iota(jnp.int32, (256, 64), 0) == where).astype(F32).astype(BF16)
            parts.append(dot(hot, patches[m, image], 0, 0))
        return jnp.concatenate(parts, axis=0).astype(BF16)

    q_far = (1 - h) * 2 + c
    mine = pl.ds(pl.multiple_of(x * 32, 32), 32)

    def far_copy(buf, send, recv, i):
        return pltpu.make_async_remote_copy(
            buf.at[:, q_far, mine], buf.at[:, q_far, mine], send.at[i], recv.at[i],
            device_id=cx_dev(i), device_id_type=MESH,
        )

    def y4_copy(buf, send, recv):
        return pltpu.make_async_remote_copy(
            buf.at[:, q, mine], buf.at[:, q, mine], send.at[8], recv.at[8],
            device_id=y4_dev, device_id_type=MESH,
        )

    def core_copy(buf, send, recv):
        return pltpu.make_async_remote_copy(
            buf.at[:, q], buf.at[:, q], send.at[0], recv.at[0],
            device_id=core_dev, device_id_type=MESH,
        )

    load_pos.wait()
    load_t.wait()
    for m in range(2):
        tx[m, pl.ds(q, 1)] = pick(tp, m)[None]
    y4_copy(tx, tx_send, tx_recv).start()
    core_copy(tx, tx_send, tx_recv).start()
    quad_copies[2].wait_recv()
    ring_start(1)
    load_s.wait()
    for m in range(2):
        sx[m, pl.ds(q, 1)] = pick(sp, m)[None]
    y4_copy(sx, sx_send, sx_recv).start()
    core_copy(sx, sx_send, sx_recv).start()

    def forward_far(buf, send, recv):
        y4_copy(buf, send, recv).wait_recv()

        def body(i, carry):
            far_copy(buf, send, recv, i).start()
            return carry

        lax.fori_loop(1, 8, body, 0)
        drain(8, 9, lambda i: y4_copy(buf, send, recv))
        drain(0, 1, lambda i: core_copy(buf, send, recv))
        drain(1, 8, lambda i: far_copy(buf, send, recv, i))

    def rows_arrive(buf, send, recv):
        core_copy(buf, send, recv).wait_recv()

        def body(i, carry):
            far_copy(buf, send, recv, i).wait_recv()
            return carry

        lax.fori_loop(1, 8, body, 0)

    quad_copies[0].wait_recv()
    ring_start(2)
    quad_copies[1].wait_recv()
    ring_start(3)
    forward_far(tx, tx_send, tx_recv)
    forward_far(sx, sx_send, sx_recv)

    rows_arrive(tx, tx_send, tx_recv)
    for m in range(2):
        for part in range(4):
            values = tx[m, part].astype(F32)
            factor = lax.rsqrt(jnp.sum(values * values, axis=1, keepdims=True) + EPSILON)
            th[m, part * 128 : part * 128 + 128, :] = (values * factor).astype(BF16)

    def ring_wait(d, carry):
        for j in range(4):
            ring_copy(j, d).wait_recv()
        return carry

    lax.fori_loop(1, 8, ring_wait, 0)

    def unpack(b, total):
        block = pg[b].astype(F32)
        rows = jnp.concatenate([block[0:8, :], block[8:16, :]], axis=1)
        pu[pl.ds(pl.multiple_of(b * 8, 8), 8), :] = rows
        return total + rows * rows

    total = lax.fori_loop(0, 32, unpack, jnp.zeros((8, 1024), F32))
    pfac[...] = jnp.broadcast_to(
        lax.rsqrt(jnp.sum(total, axis=0, keepdims=True) + EPSILON), (8, 1024)
    )

    def normalize(b, carry):
        at = pl.ds(pl.multiple_of(b * 16, 16), 16)
        unit = pu[at, :] * pfac[0:1, :]
        pu[at, :] = unit
        ph[at, :] = unit.astype(BF16)
        return carry

    lax.fori_loop(0, 16, normalize, 0)

    def tile_send(buf, send, recv, group):
        def body(d, carry):
            pltpu.make_async_remote_copy(
                buf.at[0], buf.at[d], send.at[d], recv.at[d], device_id=group(d), device_id_type=MESH
            ).start()
            return carry
        lax.fori_loop(1, 8, body, 0)
        drain(1, 8, lambda d: pltpu.make_async_remote_copy(
            buf.at[0], buf.at[d], send.at[d], recv.at[d], device_id=group(d), device_id_type=MESH
        ))

    def tile_recv(buf, send, recv, group):
        def body(d, carry):
            pltpu.make_async_remote_copy(
                buf.at[0], buf.at[d], send.at[d], recv.at[d], device_id=group(d), device_id_type=MESH
            ).wait_recv()
            return carry
        lax.fori_loop(1, 8, body, 0)
        return jnp.sum(buf[...], axis=0)

    def col_store(it, m, tile, sums):
        width = sums.shape[1] // 128
        for part in range(width):
            row = tile * width + part
            colbuf[it, m, 0, row : row + 1, :] = sums[:, part * 128 : part * 128 + 128]

    def lane_sums(block):
        return jnp.sum(block.T, axis=0, keepdims=True)

    def spread(row):
        return jnp.broadcast_to(row, (128, 128)).T

    def col_send_start(it, m):
        tile_send(colbuf.at[it, m], col_send.at[it, m], col_recv.at[it, m], z_dev)

    for m in range(2):
        for tile in range(4):
            at = slice(tile * 256, tile * 256 + 256)
            scores = dot(th[m], ph[:, at], 1, 0)
            values = jnp.exp2(scores * TEACHER_EXP2)
            kmat[m, :, at] = values
            col_store(0, m, tile, jnp.sum(values, axis=0, keepdims=True))
        col_send_start(0, m)

    for copy in quad_copies:
        copy.wait_send()

    def ring_sent(d, carry):
        for j in range(4):
            ring_copy(j, d).wait_send()
        return carry

    lax.fori_loop(1, 8, ring_sent, 0)

    rows_arrive(sx, sx_send, sx_recv)
    for m in range(2):
        for part in range(4):
            values = sx[m, part].astype(F32)
            turned = jnp.concatenate([values[:, :128].T, values[:, 128:].T], axis=0)
            factor = lax.rsqrt(jnp.sum(turned * turned, axis=0, keepdims=True) + EPSILON)
            unit = turned * factor
            at = slice(part * 128, part * 128 + 128)
            ut[m, :, at] = unit
            sht[m, :, at] = unit.astype(BF16)
            sfac[m, part] = jnp.broadcast_to(factor, (8, 128))
            sh[m, at, :] = jnp.concatenate([unit[:128, :].T, unit[128:, :].T], axis=1).astype(BF16)

    for m in range(2):
        acc = None
        for tile in range(4):
            at = slice(tile * 256, tile * 256 + 256)
            logits = dot(sh[m], ph[:, at], 1, 0)
            values = jnp.exp2(logits * STUDENT_EXP2)
            emat[m, :, at] = values
            half = values[:, :128] + values[:, 128:]
            acc = half if acc is None else acc + half
        for part in range(4):
            rowbuf1[0, m, 0, 4 + part : 5 + part, :] = lane_sums(acc[part * 128 : part * 128 + 128, :])

    load_scale.wait()
    loss_factor = scale_ref[0] * (1.0 / (2 * 4096 * 0.1))

    for it in range(ITERS):
        for m in range(2):
            total = tile_recv(colbuf.at[it, m], col_send.at[it, m], col_recv.at[it, m], z_dev)
            csc[m] = 1.0 / total
            for part in range(4):
                at = slice(part * 128, part * 128 + 128)
                acc = jnp.zeros((128, 128), F32)
                for tile in range(8):
                    acc = acc + kmat[m, at, tile * 128 : tile * 128 + 128] * csc[m, tile : tile + 1, :]
                rowbuf1[it, m, 0, part : part + 1, :] = lane_sums(acc)
            if it > 0:
                rowbuf1[it, m, 0, 4:8, :] = jnp.zeros((4, 128), F32)
            tile_send(rowbuf1.at[it, m], row1_send.at[it, m], row1_recv.at[it, m], cx_dev)
        flush()
        for m in range(2):
            total = tile_recv(rowbuf1.at[it, m], row1_send.at[it, m], row1_recv.at[it, m], cx_dev)
            rowbuf2[it, m, 0] = total
            tile_send(rowbuf2.at[it, m], row2_send.at[it, m], row2_recv.at[it, m], y_dev)
        for m in range(2):
            total = tile_recv(rowbuf2.at[it, m], row2_send.at[it, m], row2_recv.at[it, m], y_dev)
            inverse = 1.0 / total[0:4, :]
            if it == ITERS - 1:
                inverse = inverse * loss_factor
            for part in range(4):
                rb[m, part * 128 : part * 128 + 128, :] = spread(inverse[part : part + 1, :])
            if it == 0:
                denominator = loss_factor / total[4:8, :]
                for part in range(4):
                    tb[m, part * 128 : part * 128 + 128, :] = spread(denominator[part : part + 1, :])
            if it < ITERS - 1:
                for tile in range(8):
                    at = slice(tile * 128, tile * 128 + 128)
                    sums = jnp.sum(kmat[m, :, at] * rb[m], axis=0, keepdims=True)
                    col_store(it + 1, m, tile, sums)
                col_send_start(it + 1, m)

    for m in range(2):
        for tile in range(8):
            at = slice(tile * 128, tile * 128 + 128)
            target = kmat[m, :, at] * rb[m] * csc[m, tile : tile + 1, :]
            slopes[m, :, at] = (emat[m, :, at] * tb[m] - target).astype(BF16)

    for tile in range(4):
        at = slice(tile * 256, tile * 256 + 256)
        proto_sum = dot(sht[0], slopes[0, :, at], 1, 0) + dot(sht[1], slopes[1, :, at], 1, 0)
        unit = pu[:, at]
        column_dot = jnp.sum(unit * proto_sum, axis=0, keepdims=True)
        pterm[:, at] = (proto_sum - unit * column_dot) * pfac[0:1, at]

    def send_back(d, carry):
        target = lax.rem(me + d, 32)
        rows = pterm[pl.ds(pl.multiple_of(target * 8, 8), 8), :]
        packed = jnp.concatenate([rows[:, :512], rows[:, 512:]], axis=0)
        send_r[pl.ds(d, 1)] = packed.astype(BF16)[None]
        pltpu.make_async_remote_copy(
            send_r.at[d], rr.at[me], rr_send.at[d], rr_recv.at[d],
            device_id=(target, mp), device_id_type=MESH,
        ).start()
        return carry

    def rr_copy(d):
        return pltpu.make_async_remote_copy(
            send_r.at[d], rr.at[me], rr_send.at[d], rr_recv.at[d],
            device_id=(lax.rem(me + d, 32), mp), device_id_type=MESH,
        )

    lax.fori_loop(1, 32, send_back, 0)
    drain(1, 32, rr_copy)
    own = pterm[pl.ds(pl.multiple_of(me * 8, 8), 8), :]
    rr[pl.ds(me, 1)] = jnp.concatenate([own[:, :512], own[:, 512:]], axis=0).astype(BF16)[None]

    for m in range(2):
        grad = dot(ph[...], slopes[m], 1, 1)
        unit = ut[m]
        inner = jnp.sum(unit * grad, axis=0, keepdims=True)
        grad = (grad - unit * inner).astype(BF16)
        for xx in range(4):
            for part in range(4):
                lane = ((part // 2) * 2 + m) * 128
                fs[xx * 2 + part % 2, :, lane : lane + 128] = grad[
                    xx * 64 : xx * 64 + 64, part * 128 : part * 128 + 128
                ]

    def fs_copy(i):
        slot = lax.rem(x + i // 2, 4) * 2 + lax.rem(c + lax.rem(i, 2), 2)
        return pltpu.make_async_remote_copy(
            fs.at[slot], fr.at[i], fr_send.at[i], fr_recv.at[i],
            device_id=cx_dev(i), device_id_type=MESH,
        )

    def fs_start(i, carry):
        fs_copy(i).start()
        return carry

    def fs_wait(i, carry):
        fs_copy(i).wait_recv()
        return carry

    lax.fori_loop(1, 8, fs_start, 0)
    drain(1, 8, fs_copy)
    fr[pl.ds(0, 1)] = fs[pl.ds(x * 2 + c, 1)]
    lax.fori_loop(1, 8, fs_wait, 0)

    def fs_sum(l_to, carry):
        at = pl.ds(pl.multiple_of(l_to * 16, 16), 16)
        total = fr[0, at, :].astype(F32)
        for slot in range(1, 8):
            total = total + fr[slot, at, :].astype(F32)
        total = total.astype(BF16)
        gsend[pl.ds(l_to, 1)] = total[:, :256][None]
        gsend[pl.ds(4 + l_to, 1)] = total[:, 256:][None]
        return carry

    lax.fori_loop(0, 4, fs_sum, 0)

    def gr_copy(d):
        return pltpu.make_async_remote_copy(
            gsend.at[lax.rem(y + d, 8)], grecv.at[d], gr_send.at[d], gr_recv.at[d],
            device_id=y_dev(d), device_id_type=MESH,
        )

    def gr_start(d, carry):
        gr_copy(d).start()
        return carry

    def gr_wait(d, carry):
        gr_copy(d).wait_recv()
        return carry

    lax.fori_loop(1, 8, gr_start, 0)
    drain(1, 8, gr_copy)
    grecv[pl.ds(0, 1)] = gsend[pl.ds(y, 1)]
    lax.fori_loop(1, 8, gr_wait, 0)
    total = jnp.sum(grecv[...].astype(F32), axis=0)
    for m in range(2):
        gs_ref[m] = (
            total[:, m * 128 : m * 128 + 128] * sfac[m, pl.ds(q, 1)][0, 0:1, :]
        )

    def rr_wait(d, carry):
        rr_copy(d).wait_recv()
        return carry

    lax.fori_loop(1, 32, rr_wait, 0)
    for part in range(4):
        total = rr[part].astype(F32)
        for zz in range(1, 8):
            total = total + rr[zz * 4 + part].astype(F32)
        gp_ref[:, part * 1024 : part * 1024 + 512] = total[0:8, :]
        gp_ref[:, part * 1024 + 512 : part * 1024 + 1024] = total[8:16, :]

    flush()


def local(student_patches, teacher_patches, positions, prototypes, loss_scale):
    vmem = pl.BlockSpec(memory_space=pltpu.VMEM)
    hbm = pl.BlockSpec(memory_space=pltpu.HBM)
    dma = pltpu.SemaphoreType.DMA
    grad_t, grad_protos = pl.pallas_call(
        kernel,
        out_shape=(
            jax.ShapeDtypeStruct((2, 16, 128), F32),
            jax.ShapeDtypeStruct((8, 4096), F32),
        ),
        in_specs=[hbm] * 5,
        out_specs=(vmem, vmem),
        scratch_shapes=[
            pltpu.VMEM((2, 2, 256, 256), BF16),
            pltpu.VMEM((2, 2, 256, 256), BF16),
            pltpu.VMEM((2, 2, 64), jnp.int32),
            pltpu.VMEM((8, 4096), BF16),
            pltpu.SMEM((1,), F32),
            pltpu.VMEM((4, 16, 512), BF16),
            pltpu.VMEM((32, 16, 512), BF16),
            pltpu.VMEM((256, 1024), F32),
            pltpu.VMEM((256, 1024), BF16),
            pltpu.VMEM((8, 1024), F32),
            pltpu.VMEM((2, 4, 128, 256), BF16),
            pltpu.VMEM((2, 4, 128, 256), BF16),
            pltpu.VMEM((2, 512, 256), BF16),
            pltpu.VMEM((2, 512, 256), BF16),
            pltpu.VMEM((2, 256, 512), BF16),
            pltpu.VMEM((2, 256, 512), F32),
            pltpu.VMEM((2, 4, 8, 128), F32),
            pltpu.VMEM((2, 512, 1024), F32),
            pltpu.VMEM((2, 512, 1024), F32),
            pltpu.VMEM((2, 512, 1024), BF16),
            pltpu.VMEM((ITERS, 2, 8, 8, 128), F32),
            pltpu.VMEM((ITERS, 2, 8, 8, 128), F32),
            pltpu.VMEM((ITERS, 2, 8, 8, 128), F32),
            pltpu.VMEM((2, 8, 128), F32),
            pltpu.VMEM((2, 512, 128), F32),
            pltpu.VMEM((2, 512, 128), F32),
            pltpu.VMEM((32, 16, 512), BF16),
            pltpu.VMEM((32, 16, 512), BF16),
            pltpu.VMEM((256, 1024), F32),
            pltpu.VMEM((8, 64, 512), BF16),
            pltpu.VMEM((8, 64, 512), BF16),
            pltpu.VMEM((8, 16, 256), BF16),
            pltpu.VMEM((8, 16, 256), BF16),
            dma((5,)),
            dma((32,)),
            dma((32,)),
            dma((9,)),
            dma((9,)),
            dma((9,)),
            dma((9,)),
            dma((ITERS, 2, 8)),
            dma((ITERS, 2, 8)),
            dma((ITERS, 2, 8)),
            dma((ITERS, 2, 8)),
            dma((ITERS, 2, 8)),
            dma((ITERS, 2, 8)),
            dma((32,)),
            dma((32,)),
            dma((8,)),
            dma((8,)),
            dma((8,)),
            dma((8,)),
        ],
        compiler_params=pltpu.CompilerParams(
            collective_id=0, has_side_effects=True, vmem_limit_bytes=60 * 2**20
        ),
        cost_estimate=pl.CostEstimate(
            flops=2_200_000_000, bytes_accessed=2_000_000, transcendentals=2_000_000
        ),
        name="ibot_head",
    )(student_patches, teacher_patches, positions, prototypes, loss_scale)
    return jnp.transpose(grad_t, (0, 2, 1)), grad_protos


def solution(mesh):
    in_specs = (
        P(None, "rows", None, None),
        P(None, "rows", None, None),
        P(None, "rows", None),
        P("rows", "protos"),
        P(),
    )
    out_specs = (P(None, "rows", "protos"), P("rows", "protos"))
    return jax.shard_map(local, mesh=mesh, in_specs=in_specs, out_specs=out_specs, check_vma=False)
```

```python
import math

import jax
import jax.numpy as jnp
from jax import lax
from jax.experimental import pallas as pl
from jax.experimental.pallas import tpu as pltpu
from jax.sharding import PartitionSpec as P

ITERS = 3
LOG2E = 1.4426950408889634
TEACHER_EXP2 = LOG2E / 0.07
STUDENT_EXP2 = LOG2E / 0.1
EPSILON = 1e-6
MESH = pl.DeviceIdType.MESH
F32 = jnp.float32
BF16 = jnp.bfloat16


def dot(a, b, ca, cb):
    return lax.dot_general(a, b, (((ca,), (cb,)), ((), ())), preferred_element_type=F32)


def kernel(
    sp_hbm, tp_hbm, pos_hbm, pr_hbm, scale_hbm,
    gs_ref, gp_ref,
    sp, tp, pos_ref, pr_ref, scale_ref, send_p, pg, pu, ph, pfac,
    tx, sx, th, sh, sht, ut, sfac,
    kmat, emat, slopes,
    colbuf, rowbuf1, rowbuf2, csc, rb, tb,
    send_r, rr, pterm, fs, fr, gsend, grecv,
    local_sem, pg_send, pg_recv,
    tx_send, tx_recv, sx_send, sx_recv,
    col_send, col_recv, row1_send, row1_recv, row2_send, row2_recv,
    rr_send, rr_recv, fr_send, fr_recv, gr_send, gr_recv,
):
    me = lax.axis_index("rows")
    mp = lax.axis_index("protos")
    z, h, c = me // 4, lax.rem(me // 2, 2), lax.rem(me, 2)
    x, l = mp // 4, lax.rem(mp, 4)
    q = h * 2 + c
    y = h * 4 + l

    drains = []

    def drain(first, count, copy):
        def wait(i, carry):
            copy(i).wait_send()
            return carry
        drains.append((first, count, wait))

    def flush():
        for first, count, wait in drains:
            lax.fori_loop(first, count, wait, 0)
        drains.clear()

    def z_dev(d):
        return (lax.rem(z + d, 8) * 4 + q, mp)

    def cx_dev(i):
        dx, dc = i // 2, lax.rem(i, 2)
        return (z * 4 + h * 2 + lax.rem(c + dc, 2), lax.rem(x + dx, 4) * 4 + l)

    def y_dev(d):
        other = lax.rem(y + d, 8)
        return (z * 4 + (other // 4) * 2 + c, x * 4 + lax.rem(other, 4))

    core_dev = (z * 4 + h * 2 + (1 - c), mp)
    y4_dev = (z * 4 + (1 - h) * 2 + c, mp)
    diag_dev = (z * 4 + (1 - h) * 2 + (1 - c), mp)

    barrier = pltpu.get_barrier_semaphore()
    pl.semaphore_signal(barrier, inc=1, device_id=diag_dev, device_id_type=MESH)

    def greet(d, carry):
        for group in (z_dev, y_dev, cx_dev):
            pl.semaphore_signal(barrier, inc=1, device_id=group(d), device_id_type=MESH)
        return carry

    lax.fori_loop(1, 8, greet, 0)

    load_p = pltpu.make_async_copy(pr_hbm, pr_ref, local_sem.at[2])
    load_p.start()
    load_pos = pltpu.make_async_copy(pos_hbm, pos_ref, local_sem.at[3])
    load_pos.start()
    load_scale = pltpu.make_async_copy(scale_hbm, scale_ref, local_sem.at[4])
    load_scale.start()
    load_t = pltpu.make_async_copy(tp_hbm, tp, local_sem.at[0])
    load_t.start()
    load_s = pltpu.make_async_copy(sp_hbm, sp, local_sem.at[1])
    load_s.start()

    load_p.wait()
    wide = pr_ref[...].astype(F32)
    for other in range(4):
        first = wide[:, other * 1024 : other * 1024 + 512]
        second = wide[:, other * 1024 + 512 : other * 1024 + 1024]
        send_p[other] = jnp.concatenate([first, second], axis=0).astype(BF16)
    pg[pl.ds(me, 1)] = send_p[pl.ds(q, 1)]

    pl.semaphore_wait(barrier, 22)

    def relative(j):
        return (h + (j // 2)) % 2 * 2 + (c + j % 2) % 2

    def quad_copy(j, target):
        return pltpu.make_async_remote_copy(
            send_p.at[relative(j)], pg.at[me], pg_send.at[j], pg_recv.at[j],
            device_id=target, device_id_type=MESH,
        )

    quad_copies = [quad_copy(2, y4_dev), quad_copy(3, diag_dev), quad_copy(1, core_dev)]

    def ring_copy(j, d):
        at = z * 4 + relative(j)
        return pltpu.make_async_remote_copy(
            pg.at[at], pg.at[at], pg_send.at[d * 4 + j], pg_recv.at[d * 4 + j],
            device_id=z_dev(d), device_id_type=MESH,
        )

    def ring_start(j):
        for d in (4, 5, 3, 6, 2, 7, 1):
            ring_copy(j, d).start()

    for copy in quad_copies:
        copy.start()
    ring_start(0)

    def pick(patches, m):
        parts = []
        for image in range(2):
            where = jnp.broadcast_to(pos_ref[m, image : image + 1, :], (256, 64))
            hot = (lax.broadcasted_iota(jnp.int32, (256, 64), 0) == where).astype(F32).astype(BF16)
            parts.append(dot(hot, patches[m, image], 0, 0))
        return jnp.concatenate(parts, axis=0).astype(BF16)

    q_far = (1 - h) * 2 + c
    mine = pl.ds(pl.multiple_of(x * 32, 32), 32)

    def far_copy(buf, send, recv, i):
        return pltpu.make_async_remote_copy(
            buf.at[:, q_far, mine], buf.at[:, q_far, mine], send.at[i], recv.at[i],
            device_id=cx_dev(i), device_id_type=MESH,
        )

    def y4_copy(buf, send, recv):
        return pltpu.make_async_remote_copy(
            buf.at[:, q, mine], buf.at[:, q, mine], send.at[8], recv.at[8],
            device_id=y4_dev, device_id_type=MESH,
        )

    def core_copy(buf, send, recv):
        return pltpu.make_async_remote_copy(
            buf.at[:, q], buf.at[:, q], send.at[0], recv.at[0],
            device_id=core_dev, device_id_type=MESH,
        )

    load_pos.wait()
    load_t.wait()
    for m in range(2):
        tx[m, pl.ds(q, 1)] = pick(tp, m)[None]
    y4_copy(tx, tx_send, tx_recv).start()
    core_copy(tx, tx_send, tx_recv).start()
    quad_copies[2].wait_recv()
    ring_start(1)
    load_s.wait()
    for m in range(2):
        sx[m, pl.ds(q, 1)] = pick(sp, m)[None]
    y4_copy(sx, sx_send, sx_recv).start()
    core_copy(sx, sx_send, sx_recv).start()

    def forward_far(buf, send, recv):
        y4_copy(buf, send, recv).wait_recv()

        def body(i, carry):
            far_copy(buf, send, recv, i).start()
            return carry

        lax.fori_loop(1, 8, body, 0)
        drain(8, 9, lambda i: y4_copy(buf, send, recv))
        drain(0, 1, lambda i: core_copy(buf, send, recv))
        drain(1, 8, lambda i: far_copy(buf, send, recv, i))

    def rows_arrive(buf, send, recv):
        core_copy(buf, send, recv).wait_recv()

        def body(i, carry):
            far_copy(buf, send, recv, i).wait_recv()
            return carry

        lax.fori_loop(1, 8, body, 0)

    quad_copies[0].wait_recv()
    ring_start(2)
    quad_copies[1].wait_recv()
    ring_start(3)
    forward_far(tx, tx_send, tx_recv)
    forward_far(sx, sx_send, sx_recv)

    rows_arrive(tx, tx_send, tx_recv)
    for m in range(2):
        for part in range(4):
            values = tx[m, part].astype(F32)
            factor = lax.rsqrt(jnp.sum(values * values, axis=1, keepdims=True) + EPSILON)
            th[m, part * 128 : part * 128 + 128, :] = (values * factor).astype(BF16)

    def ring_wait(d, first):
        for j in range(2):
            ring_copy(first + j, d).wait_recv()
        return first

    def unpack_half(half):
        def unpack(i, total):
            b = i // 2 * 4 + half * 2 + lax.rem(i, 2)
            block = pg[b].astype(F32)
            rows = jnp.concatenate([block[0:8, :], block[8:16, :]], axis=1)
            pu[pl.ds(pl.multiple_of(b * 8, 8), 8), :] = rows
            return total + rows * rows
        return unpack

    lax.fori_loop(1, 8, ring_wait, 0)
    total = lax.fori_loop(0, 16, unpack_half(h), jnp.zeros((8, 1024), F32))
    lax.fori_loop(1, 8, ring_wait, 2)
    total = lax.fori_loop(0, 16, unpack_half(1 - h), total)
    pfac[...] = jnp.broadcast_to(
        lax.rsqrt(jnp.sum(total, axis=0, keepdims=True) + EPSILON), (8, 1024)
    )

    def normalize(b, carry):
        at = pl.ds(pl.multiple_of(b * 16, 16), 16)
        unit = pu[at, :] * pfac[0:1, :]
        pu[at, :] = unit
        ph[at, :] = unit.astype(BF16)
        return carry

    lax.fori_loop(0, 16, normalize, 0)

    ring_order = (4, 5, 3, 6, 2, 7, 1)
    cx_order = (4, 5, 2, 3, 6, 7, 1)

    def tile_copy(buf, send, recv, device, d):
        return pltpu.make_async_remote_copy(
            buf.at[0], buf.at[d], send.at[d], recv, device_id=device, device_id_type=MESH
        )

    def tile_send(buf, send, recv, group):
        devices, order = group
        for d in order:
            tile_copy(buf, send, recv, devices[d], d).start()
        drain(1, 8, lambda d: tile_copy(buf, send, recv, core_dev, d))

    def tile_recv(buf, recv):
        pltpu.make_async_copy(buf.at[pl.ds(1, 7)], buf.at[pl.ds(1, 7)], recv).wait()
        return jnp.sum(buf[...], axis=0)

    z_group = ([z_dev(d) for d in range(8)], ring_order)
    y_group = ([y_dev(d) for d in range(8)], ring_order)
    cx_group = ([cx_dev(d) for d in range(8)], cx_order)

    def col_store(it, m, tile, sums):
        width = sums.shape[1] // 128
        for part in range(width):
            row = tile * width + part
            colbuf[it, m, 0, row : row + 1, :] = sums[:, part * 128 : part * 128 + 128]

    def lane_sums(block):
        return jnp.sum(block.T, axis=0, keepdims=True)

    def spread(row):
        return jnp.broadcast_to(row, (128, 128)).T

    def col_send_start(it, m):
        tile_send(colbuf.at[it, m], col_send.at[it, m], col_recv.at[it, m], z_group)

    for m in range(2):
        for tile in range(4):
            at = slice(tile * 256, tile * 256 + 256)
            scores = dot(th[m], ph[:, at], 1, 0)
            values = jnp.exp2(scores * TEACHER_EXP2)
            kmat[m, :, at] = values
            col_store(0, m, tile, jnp.sum(values, axis=0, keepdims=True))
        col_send_start(0, m)

    for copy in quad_copies:
        copy.wait_send()

    def ring_sent(d, carry):
        for j in range(4):
            ring_copy(j, d).wait_send()
        return carry

    lax.fori_loop(1, 8, ring_sent, 0)

    rows_arrive(sx, sx_send, sx_recv)
    for m in range(2):
        for part in range(4):
            values = sx[m, part].astype(F32)
            turned = jnp.concatenate([values[:, :128].T, values[:, 128:].T], axis=0)
            factor = lax.rsqrt(jnp.sum(turned * turned, axis=0, keepdims=True) + EPSILON)
            unit = turned * factor
            at = slice(part * 128, part * 128 + 128)
            ut[m, :, at] = unit
            sht[m, :, at] = unit.astype(BF16)
            sfac[m, part] = jnp.broadcast_to(factor, (8, 128))
            sh[m, at, :] = jnp.concatenate([unit[:128, :].T, unit[128:, :].T], axis=1).astype(BF16)

    for m in range(2):
        acc = None
        for tile in range(4):
            at = slice(tile * 256, tile * 256 + 256)
            logits = dot(sh[m], ph[:, at], 1, 0)
            values = jnp.exp2(logits * STUDENT_EXP2)
            emat[m, :, at] = values
            half = values[:, :128] + values[:, 128:]
            acc = half if acc is None else acc + half
        for part in range(4):
            rowbuf1[0, m, 0, 4 + part : 5 + part, :] = lane_sums(acc[part * 128 : part * 128 + 128, :])

    load_scale.wait()
    loss_factor = scale_ref[0] * (1.0 / (2 * 4096 * 0.1))

    for it in range(ITERS):
        for m in range(2):
            total = tile_recv(colbuf.at[it, m], col_recv.at[it, m])
            csc[m] = 1.0 / total
            for part in range(4):
                at = slice(part * 128, part * 128 + 128)
                acc = jnp.zeros((128, 128), F32)
                for tile in range(8):
                    acc = acc + kmat[m, at, tile * 128 : tile * 128 + 128] * csc[m, tile : tile + 1, :]
                rowbuf1[it, m, 0, part : part + 1, :] = lane_sums(acc)
            if it > 0:
                rowbuf1[it, m, 0, 4:8, :] = jnp.zeros((4, 128), F32)
            tile_send(rowbuf1.at[it, m], row1_send.at[it, m], row1_recv.at[it, m], cx_group)
        flush()
        if it == 1:
            for m in range(2):
                for tile in range(8):
                    at = slice(tile * 128, tile * 128 + 128)
                    emat[m, :, at] = emat[m, :, at] * tb[m]
        if it == ITERS - 1:
            for m in range(2):
                for tile in range(8):
                    at = slice(tile * 128, tile * 128 + 128)
                    kmat[m, :, at] = kmat[m, :, at] * csc[m, tile : tile + 1, :]
        for m in range(2):
            total = tile_recv(rowbuf1.at[it, m], row1_recv.at[it, m])
            rowbuf2[it, m, 0] = total
            tile_send(rowbuf2.at[it, m], row2_send.at[it, m], row2_recv.at[it, m], y_group)
        for m in range(2):
            total = tile_recv(rowbuf2.at[it, m], row2_recv.at[it, m])
            inverse = 1.0 / total[0:4, :]
            if it == ITERS - 1:
                inverse = inverse * loss_factor
            for part in range(4):
                rb[m, part * 128 : part * 128 + 128, :] = spread(inverse[part : part + 1, :])
            if it == 0:
                denominator = loss_factor / total[4:8, :]
                for part in range(4):
                    tb[m, part * 128 : part * 128 + 128, :] = spread(denominator[part : part + 1, :])
            if it < ITERS - 1:
                for tile in range(8):
                    at = slice(tile * 128, tile * 128 + 128)
                    sums = jnp.sum(kmat[m, :, at] * rb[m], axis=0, keepdims=True)
                    col_store(it + 1, m, tile, sums)
                col_send_start(it + 1, m)

    for m in range(2):
        for tile in range(8):
            at = slice(tile * 128, tile * 128 + 128)
            slopes[m, :, at] = (emat[m, :, at] - kmat[m, :, at] * rb[m]).astype(BF16)

    for tile in range(4):
        at = slice(tile * 256, tile * 256 + 256)
        proto_sum = dot(sht[0], slopes[0, :, at], 1, 0) + dot(sht[1], slopes[1, :, at], 1, 0)
        unit = pu[:, at]
        column_dot = jnp.sum(unit * proto_sum, axis=0, keepdims=True)
        pterm[:, at] = (proto_sum - unit * column_dot) * pfac[0:1, at]

    def send_back(d, carry):
        target = lax.rem(me + d, 32)
        rows = pterm[pl.ds(pl.multiple_of(target * 8, 8), 8), :]
        packed = jnp.concatenate([rows[:, :512], rows[:, 512:]], axis=0)
        send_r[pl.ds(d, 1)] = packed.astype(BF16)[None]
        pltpu.make_async_remote_copy(
            send_r.at[d], rr.at[me], rr_send.at[d], rr_recv.at[d],
            device_id=(target, mp), device_id_type=MESH,
        ).start()
        return carry

    def back_to(i):
        step = i // 4
        dz = lax.rem(4 + (step + 1) // 2 * (2 * lax.rem(step, 2) - 1), 8)
        j = 3 - lax.rem(i, 4)
        q_to = lax.rem(h + j // 2, 2) * 2 + lax.rem(c + lax.rem(j, 2), 2)
        return lax.rem(z + dz, 8) * 4 + q_to

    def rr_copy(i):
        return pltpu.make_async_remote_copy(
            send_r.at[i], rr.at[me], rr_send.at[i], rr_recv.at[i],
            device_id=(back_to(i), mp), device_id_type=MESH,
        )

    def send_back(i, carry):
        rows = pterm[pl.ds(pl.multiple_of(back_to(i) * 8, 8), 8), :]
        packed = jnp.concatenate([rows[:, :512], rows[:, 512:]], axis=0)
        send_r[pl.ds(i, 1)] = packed.astype(BF16)[None]
        rr_copy(i).start()
        return carry

    lax.fori_loop(0, 31, send_back, 0)
    drain(0, 31, rr_copy)
    own = pterm[pl.ds(pl.multiple_of(me * 8, 8), 8), :]
    rr[pl.ds(me, 1)] = jnp.concatenate([own[:, :512], own[:, 512:]], axis=0).astype(BF16)[None]

    for m in range(2):
        grad = dot(ph[...], slopes[m], 1, 1)
        unit = ut[m]
        inner = jnp.sum(unit * grad, axis=0, keepdims=True)
        grad = (grad - unit * inner).astype(BF16)
        for xx in range(4):
            for part in range(4):
                lane = ((part // 2) * 2 + m) * 128
                fs[xx * 2 + part % 2, :, lane : lane + 128] = grad[
                    xx * 64 : xx * 64 + 64, part * 128 : part * 128 + 128
                ]

    def fs_copy(i):
        slot = lax.rem(x + i // 2, 4) * 2 + lax.rem(c + lax.rem(i, 2), 2)
        return pltpu.make_async_remote_copy(
            fs.at[slot], fr.at[i], fr_send.at[i], fr_recv.at[i],
            device_id=cx_dev(i), device_id_type=MESH,
        )

    def fs_start(i, carry):
        fs_copy(i).start()
        return carry

    def fs_wait(i, carry):
        fs_copy(i).wait_recv()
        return carry

    lax.fori_loop(1, 8, fs_start, 0)
    drain(1, 8, fs_copy)
    fr[pl.ds(0, 1)] = fs[pl.ds(x * 2 + c, 1)]
    lax.fori_loop(1, 8, fs_wait, 0)

    def fs_sum(l_to, carry):
        at = pl.ds(pl.multiple_of(l_to * 16, 16), 16)
        total = fr[0, at, :].astype(F32)
        for slot in range(1, 8):
            total = total + fr[slot, at, :].astype(F32)
        total = total.astype(BF16)
        gsend[pl.ds(l_to, 1)] = total[:, :256][None]
        gsend[pl.ds(4 + l_to, 1)] = total[:, 256:][None]
        return carry

    lax.fori_loop(0, 4, fs_sum, 0)

    def gr_copy(d):
        return pltpu.make_async_remote_copy(
            gsend.at[lax.rem(y + d, 8)], grecv.at[d], gr_send.at[d], gr_recv.at[d],
            device_id=y_dev(d), device_id_type=MESH,
        )

    def gr_start(d, carry):
        gr_copy(d).start()
        return carry

    def gr_wait(d, carry):
        gr_copy(d).wait_recv()
        return carry

    lax.fori_loop(1, 8, gr_start, 0)
    drain(1, 8, gr_copy)
    grecv[pl.ds(0, 1)] = gsend[pl.ds(y, 1)]
    lax.fori_loop(1, 8, gr_wait, 0)
    total = jnp.sum(grecv[...].astype(F32), axis=0)
    for m in range(2):
        gs_ref[m] = (
            total[:, m * 128 : m * 128 + 128] * sfac[m, pl.ds(q, 1)][0, 0:1, :]
        )

    def rr_wait(d, carry):
        rr_copy(d).wait_recv()
        return carry

    flush()
    lax.fori_loop(0, 31, rr_wait, 0)
    for part in range(4):
        total = rr[part].astype(F32)
        for zz in range(1, 8):
            total = total + rr[zz * 4 + part].astype(F32)
        gp_ref[:, part * 1024 : part * 1024 + 512] = total[0:8, :]
        gp_ref[:, part * 1024 + 512 : part * 1024 + 1024] = total[8:16, :]

    flush()


def local(student_patches, teacher_patches, positions, prototypes, loss_scale):
    vmem = pl.BlockSpec(memory_space=pltpu.VMEM)
    hbm = pl.BlockSpec(memory_space=pltpu.HBM)
    dma = pltpu.SemaphoreType.DMA
    grad_t, grad_protos = pl.pallas_call(
        kernel,
        out_shape=(
            pltpu.VMEM((2, 16, 128), F32),
            pltpu.VMEM((8, 4096), F32),
        ),
        in_specs=[hbm] * 5,
        out_specs=(vmem, vmem),
        scratch_shapes=[
            pltpu.VMEM((2, 2, 256, 256), BF16),
            pltpu.VMEM((2, 2, 256, 256), BF16),
            pltpu.VMEM((2, 2, 64), jnp.int32),
            pltpu.VMEM((8, 4096), BF16),
            pltpu.SMEM((1,), F32),
            pltpu.VMEM((4, 16, 512), BF16),
            pltpu.VMEM((32, 16, 512), BF16),
            pltpu.VMEM((256, 1024), F32),
            pltpu.VMEM((256, 1024), BF16),
            pltpu.VMEM((8, 1024), F32),
            pltpu.VMEM((2, 4, 128, 256), BF16),
            pltpu.VMEM((2, 4, 128, 256), BF16),
            pltpu.VMEM((2, 512, 256), BF16),
            pltpu.VMEM((2, 512, 256), BF16),
            pltpu.VMEM((2, 256, 512), BF16),
            pltpu.VMEM((2, 256, 512), F32),
            pltpu.VMEM((2, 4, 8, 128), F32),
            pltpu.VMEM((2, 512, 1024), F32),
            pltpu.VMEM((2, 512, 1024), F32),
            pltpu.VMEM((2, 512, 1024), BF16),
            pltpu.VMEM((ITERS, 2, 8, 8, 128), F32),
            pltpu.VMEM((ITERS, 2, 8, 8, 128), F32),
            pltpu.VMEM((ITERS, 2, 8, 8, 128), F32),
            pltpu.VMEM((2, 8, 128), F32),
            pltpu.VMEM((2, 512, 128), F32),
            pltpu.VMEM((2, 512, 128), F32),
            pltpu.VMEM((32, 16, 512), BF16),
            pltpu.VMEM((32, 16, 512), BF16),
            pltpu.VMEM((256, 1024), F32),
            pltpu.VMEM((8, 64, 512), BF16),
            pltpu.VMEM((8, 64, 512), BF16),
            pltpu.VMEM((8, 16, 256), BF16),
            pltpu.VMEM((8, 16, 256), BF16),
            dma((5,)),
            dma((32,)),
            dma((32,)),
            dma((9,)),
            dma((9,)),
            dma((9,)),
            dma((9,)),
            dma((ITERS, 2, 8)),
            dma((ITERS, 2)),
            dma((ITERS, 2, 8)),
            dma((ITERS, 2)),
            dma((ITERS, 2, 8)),
            dma((ITERS, 2)),
            dma((32,)),
            dma((32,)),
            dma((8,)),
            dma((8,)),
            dma((8,)),
            dma((8,)),
        ],
        compiler_params=pltpu.CompilerParams(
            collective_id=0, has_side_effects=True, vmem_limit_bytes=60 * 2**20
        ),
        cost_estimate=pl.CostEstimate(
            flops=2_200_000_000, bytes_accessed=2_000_000, transcendentals=2_000_000
        ),
        name="ibot_head",
    )(student_patches, teacher_patches, positions, prototypes, loss_scale)
    return jnp.transpose(grad_t, (0, 2, 1)), grad_protos


def solution(mesh):
    in_specs = (
        P(None, "rows", None, None),
        P(None, "rows", None, None),
        P(None, "rows", None),
        P("rows", "protos"),
        P(),
    )
    out_specs = (P(None, "rows", "protos"), P("rows", "protos"))
    return jax.shard_map(local, mesh=mesh, in_specs=in_specs, out_specs=out_specs, check_vma=False)
```

```python
import math

import jax
import jax.numpy as jnp
from jax import lax
from jax.experimental import pallas as pl
from jax.experimental.pallas import tpu as pltpu
from jax.sharding import PartitionSpec as P

ITERS = 3
LOG2E = 1.4426950408889634
TEACHER_EXP2 = LOG2E / 0.07
STUDENT_EXP2 = LOG2E / 0.1
EPSILON = 1e-6
MESH = pl.DeviceIdType.MESH
F32 = jnp.float32
BF16 = jnp.bfloat16


def dot(a, b, ca, cb):
    return lax.dot_general(a, b, (((ca,), (cb,)), ((), ())), preferred_element_type=F32)


def kernel(
    sp_hbm, tp_hbm, pos_hbm, pr_hbm,
    gs_ref, gp_ref,
    sp, tp, pos_ref, pr_ref, send_p, pg, pu, ph, pfac,
    tx, sx, th, sh, sht, ut, sfac,
    kmat, emat, slopes,
    colbuf, rowbuf1, rowbuf2, csc, rb, tb,
    send_r, rr, pterm, fs, fr, gsend, grecv,
    local_sem, pg_send, pg_recv, ring_recv,
    tx_send, tx_recv, sx_send, sx_recv,
    col_send, col_recv, row1_send, row1_recv, row2_send, row2_recv,
    rr_send, rr_recv, fr_send, fr_recv, gr_send, gr_recv,
):
    me = lax.axis_index("rows")
    mp = lax.axis_index("protos")
    z, h, c = me // 4, lax.rem(me // 2, 2), lax.rem(me, 2)
    x, l = mp // 4, lax.rem(mp, 4)
    q = h * 2 + c
    y = h * 4 + l

    def take(ref, sem):
        pltpu.make_async_copy(ref, ref, sem).wait()

    def z_dev(d):
        return (lax.rem(z + d, 8) * 4 + q, mp)

    def cx_dev(i):
        dx, dc = i // 2, lax.rem(i, 2)
        return (z * 4 + h * 2 + lax.rem(c + dc, 2), lax.rem(x + dx, 4) * 4 + l)

    def y_dev(d):
        other = lax.rem(y + d, 8)
        return (z * 4 + (other // 4) * 2 + c, x * 4 + lax.rem(other, 4))

    core_dev = (z * 4 + h * 2 + (1 - c), mp)
    y4_dev = (z * 4 + (1 - h) * 2 + c, mp)
    diag_dev = (z * 4 + (1 - h) * 2 + (1 - c), mp)

    barrier = pltpu.get_barrier_semaphore()
    pl.semaphore_signal(barrier, inc=1, device_id=diag_dev, device_id_type=MESH)

    def greet(d, carry):
        for group in (z_dev, y_dev, cx_dev):
            pl.semaphore_signal(barrier, inc=1, device_id=group(d), device_id_type=MESH)
        return carry

    lax.fori_loop(1, 8, greet, 0)

    load_p = pltpu.make_async_copy(pr_hbm, pr_ref, local_sem.at[2])
    load_p.start()
    load_pos = pltpu.make_async_copy(pos_hbm, pos_ref, local_sem.at[3])
    load_pos.start()
    load_t = pltpu.make_async_copy(tp_hbm, tp, local_sem.at[0])
    load_t.start()
    load_s = pltpu.make_async_copy(sp_hbm, sp, local_sem.at[1])
    load_s.start()

    load_p.wait()
    wide = pr_ref[...].astype(F32)
    for other in range(4):
        first = wide[:, other * 1024 : other * 1024 + 512]
        second = wide[:, other * 1024 + 512 : other * 1024 + 1024]
        send_p[other] = jnp.concatenate([first, second], axis=0).astype(BF16)
    pg[pl.ds(me, 1)] = send_p[pl.ds(q, 1)]

    pl.semaphore_wait(barrier, 22)

    def relative(j):
        return (h + (j // 2)) % 2 * 2 + (c + j % 2) % 2

    def quad_copy(j, target):
        return pltpu.make_async_remote_copy(
            send_p.at[relative(j)], pg.at[me], pg_send, pg_recv.at[j],
            device_id=target, device_id_type=MESH,
        )

    quad_copies = [quad_copy(2, y4_dev), quad_copy(3, diag_dev), quad_copy(1, core_dev)]

    def ring_copy(j, d):
        at = z * 4 + relative(j)
        return pltpu.make_async_remote_copy(
            pg.at[at], pg.at[at], pg_send, ring_recv.at[j // 2],
            device_id=z_dev(d), device_id_type=MESH,
        )

    def ring_start(j):
        for d in (4, 5, 3, 6, 2, 7, 1):
            ring_copy(j, d).start()

    for copy in quad_copies:
        copy.start()
    ring_start(0)

    def pick(patches, m):
        parts = []
        for image in range(2):
            where = jnp.broadcast_to(pos_ref[m, image : image + 1, :], (256, 64))
            hot = (lax.broadcasted_iota(jnp.int32, (256, 64), 0) == where).astype(F32).astype(BF16)
            parts.append(dot(hot, patches[m, image], 0, 0))
        return jnp.concatenate(parts, axis=0).astype(BF16)

    q_far = (1 - h) * 2 + c
    mine = pl.ds(pl.multiple_of(x * 32, 32), 32)

    def far_copy(buf, send, recv, i):
        return pltpu.make_async_remote_copy(
            buf.at[:, q_far, mine], buf.at[:, q_far, mine], send, recv.at[2],
            device_id=cx_dev(i), device_id_type=MESH,
        )

    def y4_copy(buf, send, recv):
        return pltpu.make_async_remote_copy(
            buf.at[:, q, mine], buf.at[:, q, mine], send, recv.at[1],
            device_id=y4_dev, device_id_type=MESH,
        )

    def core_copy(buf, send, recv):
        return pltpu.make_async_remote_copy(
            buf.at[:, q], buf.at[:, q], send, recv.at[0],
            device_id=core_dev, device_id_type=MESH,
        )

    load_pos.wait()
    load_t.wait()
    for m in range(2):
        tx[m, pl.ds(q, 1)] = pick(tp, m)[None]
    y4_copy(tx, tx_send, tx_recv).start()
    core_copy(tx, tx_send, tx_recv).start()
    quad_copies[2].wait_recv()
    ring_start(1)
    load_s.wait()
    for m in range(2):
        sx[m, pl.ds(q, 1)] = pick(sp, m)[None]
    y4_copy(sx, sx_send, sx_recv).start()
    core_copy(sx, sx_send, sx_recv).start()

    def forward_far(buf, send, recv):
        y4_copy(buf, send, recv).wait_recv()

        def body(i, carry):
            far_copy(buf, send, recv, i).start()
            return carry

        lax.fori_loop(1, 8, body, 0)

    def rows_arrive(buf, send, recv):
        core_copy(buf, send, recv).wait_recv()
        take(buf.at[:, pl.ds(0, 2), pl.ds(0, 112)], recv.at[2])

    quad_copies[0].wait_recv()
    ring_start(2)
    quad_copies[1].wait_recv()
    ring_start(3)
    forward_far(tx, tx_send, tx_recv)
    forward_far(sx, sx_send, sx_recv)

    rows_arrive(tx, tx_send, tx_recv)
    for m in range(2):
        for part in range(4):
            values = tx[m, part].astype(F32)
            factor = lax.rsqrt(jnp.sum(values * values, axis=1, keepdims=True) + EPSILON)
            th[m, part * 128 : part * 128 + 128, :] = (values * factor).astype(BF16)

    def unpack_half(half):
        def unpack(i, total):
            b = i // 2 * 4 + half * 2 + lax.rem(i, 2)
            block = pg[b].astype(F32)
            rows = jnp.concatenate([block[0:8, :], block[8:16, :]], axis=1)
            pu[pl.ds(pl.multiple_of(b * 8, 8), 8), :] = rows
            return total + rows * rows
        return unpack

    take(pg.at[pl.ds(0, 14)], ring_recv.at[0])
    total = lax.fori_loop(0, 16, unpack_half(h), jnp.zeros((8, 1024), F32))
    take(pg.at[pl.ds(0, 14)], ring_recv.at[1])
    total = lax.fori_loop(0, 16, unpack_half(1 - h), total)
    pfac[...] = jnp.broadcast_to(
        lax.rsqrt(jnp.sum(total, axis=0, keepdims=True) + EPSILON), (8, 1024)
    )

    def normalize(b, carry):
        at = pl.ds(pl.multiple_of(b * 16, 16), 16)
        unit = pu[at, :] * pfac[0:1, :]
        pu[at, :] = unit
        ph[at, :] = unit.astype(BF16)
        return carry

    lax.fori_loop(0, 16, normalize, 0)

    ring_order = (4, 5, 3, 6, 2, 7, 1)
    cx_order = (4, 5, 2, 3, 6, 7, 1)

    def tile_send(buf, it, m, send, recv, group):
        devices, order = group
        for d in order:
            pltpu.make_async_remote_copy(
                buf.at[0, it, m], buf.at[d, it, m], send, recv.at[it, m],
                device_id=devices[d], device_id_type=MESH,
            ).start()

    def tile_recv(buf, it, m, recv):
        take(buf.at[pl.ds(1, 7), it, m], recv.at[it, m])
        return jnp.sum(buf[:, it, m], axis=0)

    z_group = ([z_dev(d) for d in range(8)], ring_order)
    y_group = ([y_dev(d) for d in range(8)], ring_order)
    cx_group = ([cx_dev(d) for d in range(8)], cx_order)

    def col_store(it, m, tile, sums):
        width = sums.shape[1] // 128
        for part in range(width):
            row = tile * width + part
            colbuf[0, it, m, row : row + 1, :] = sums[:, part * 128 : part * 128 + 128]

    def lane_sums(block):
        return jnp.sum(block.T, axis=0, keepdims=True)

    def spread(row):
        return jnp.broadcast_to(row, (128, 128)).T

    def col_send_start(it, m):
        tile_send(colbuf, it, m, col_send, col_recv, z_group)

    for m in range(2):
        for tile in range(4):
            at = slice(tile * 256, tile * 256 + 256)
            scores = dot(th[m], ph[:, at], 1, 0)
            values = jnp.exp2(scores * TEACHER_EXP2)
            kmat[m, :, at] = values
            col_store(0, m, tile, jnp.sum(values, axis=0, keepdims=True))
        col_send_start(0, m)

    rows_arrive(sx, sx_send, sx_recv)
    for m in range(2):
        for part in range(4):
            values = sx[m, part].astype(F32)
            turned = jnp.concatenate([values[:, :128].T, values[:, 128:].T], axis=0)
            factor = lax.rsqrt(jnp.sum(turned * turned, axis=0, keepdims=True) + EPSILON)
            unit = turned * factor
            at = slice(part * 128, part * 128 + 128)
            ut[m, :, at] = unit
            sht[m, :, at] = unit.astype(BF16)
            sfac[m, part] = jnp.broadcast_to(factor, (8, 128))
            sh[m, at, :] = jnp.concatenate([unit[:128, :].T, unit[128:, :].T], axis=1).astype(BF16)

    for m in range(2):
        acc = None
        for tile in range(4):
            at = slice(tile * 256, tile * 256 + 256)
            logits = dot(sh[m], ph[:, at], 1, 0)
            values = jnp.exp2(logits * STUDENT_EXP2)
            emat[m, :, at] = values
            half = values[:, :128] + values[:, 128:]
            acc = half if acc is None else acc + half
        for part in range(4):
            rowbuf1[0, 0, m, 4 + part : 5 + part, :] = lane_sums(acc[part * 128 : part * 128 + 128, :])

    for it in range(ITERS):
        for m in range(2):
            total = tile_recv(colbuf, it, m, col_recv)
            csc[m] = 1.0 / total
            for part in range(4):
                at = slice(part * 128, part * 128 + 128)
                acc = jnp.zeros((128, 128), F32)
                for tile in range(8):
                    acc = acc + kmat[m, at, tile * 128 : tile * 128 + 128] * csc[m, tile : tile + 1, :]
                rowbuf1[0, it, m, part : part + 1, :] = lane_sums(acc)
            if it > 0:
                rowbuf1[0, it, m, 4:8, :] = jnp.zeros((4, 128), F32)
            tile_send(rowbuf1, it, m, row1_send, row1_recv, cx_group)
        if it == 1:
            for m in range(2):
                for tile in range(8):
                    at = slice(tile * 128, tile * 128 + 128)
                    emat[m, :, at] = emat[m, :, at] * tb[m]
        if it == ITERS - 1:
            for m in range(2):
                for tile in range(8):
                    at = slice(tile * 128, tile * 128 + 128)
                    kmat[m, :, at] = kmat[m, :, at] * csc[m, tile : tile + 1, :]
        for m in range(2):
            total = tile_recv(rowbuf1, it, m, row1_recv)
            rowbuf2[0, it, m] = total
            tile_send(rowbuf2, it, m, row2_send, row2_recv, y_group)
        for m in range(2):
            total = tile_recv(rowbuf2, it, m, row2_recv)
            inverse = 1.0 / total[0:4, :]
            for part in range(4):
                rb[m, part * 128 : part * 128 + 128, :] = spread(inverse[part : part + 1, :])
            if it == 0:
                denominator = 1.0 / total[4:8, :]
                for part in range(4):
                    tb[m, part * 128 : part * 128 + 128, :] = spread(denominator[part : part + 1, :])
            if it < ITERS - 1:
                for tile in range(8):
                    at = slice(tile * 128, tile * 128 + 128)
                    sums = jnp.sum(kmat[m, :, at] * rb[m], axis=0, keepdims=True)
                    col_store(it + 1, m, tile, sums)
                col_send_start(it + 1, m)

    for m in range(2):
        for tile in range(8):
            at = slice(tile * 128, tile * 128 + 128)
            slopes[m, :, at] = (emat[m, :, at] - kmat[m, :, at] * rb[m]).astype(BF16)

    for tile in range(4):
        at = slice(tile * 256, tile * 256 + 256)
        proto_sum = dot(sht[0], slopes[0, :, at], 1, 0) + dot(sht[1], slopes[1, :, at], 1, 0)
        unit = pu[:, at]
        column_dot = jnp.sum(unit * proto_sum, axis=0, keepdims=True)
        pterm[:, at] = (proto_sum - unit * column_dot) * pfac[0:1, at]

    def send_back(d, carry):
        target = lax.rem(me + d, 32)
        rows = pterm[pl.ds(pl.multiple_of(target * 8, 8), 8), :]
        packed = jnp.concatenate([rows[:, :512], rows[:, 512:]], axis=0)
        send_r[pl.ds(d, 1)] = packed.astype(BF16)[None]
        pltpu.make_async_remote_copy(
            send_r.at[d], rr.at[me], rr_send.at[d], rr_recv.at[d],
            device_id=(target, mp), device_id_type=MESH,
        ).start()
        return carry

    def back_to(i):
        step = i // 4
        dz = lax.rem(4 + (step + 1) // 2 * (2 * lax.rem(step, 2) - 1), 8)
        j = 3 - lax.rem(i, 4)
        q_to = lax.rem(h + j // 2, 2) * 2 + lax.rem(c + lax.rem(j, 2), 2)
        return lax.rem(z + dz, 8) * 4 + q_to

    def rr_copy(i):
        return pltpu.make_async_remote_copy(
            send_r.at[i], rr.at[me], rr_send, rr_recv,
            device_id=(back_to(i), mp), device_id_type=MESH,
        )

    def send_back(i, carry):
        rows = pterm[pl.ds(pl.multiple_of(back_to(i) * 8, 8), 8), :]
        packed = jnp.concatenate([rows[:, :512], rows[:, 512:]], axis=0)
        send_r[pl.ds(i, 1)] = packed.astype(BF16)[None]
        rr_copy(i).start()
        return carry

    lax.fori_loop(0, 31, send_back, 0)
    own = pterm[pl.ds(pl.multiple_of(me * 8, 8), 8), :]
    rr[pl.ds(me, 1)] = jnp.concatenate([own[:, :512], own[:, 512:]], axis=0).astype(BF16)[None]

    for m in range(2):
        grad = dot(ph[...], slopes[m], 1, 1)
        unit = ut[m]
        inner = jnp.sum(unit * grad, axis=0, keepdims=True)
        grad = (grad - unit * inner).astype(BF16)
        for xx in range(4):
            for part in range(4):
                lane = ((part // 2) * 2 + m) * 128
                fs[xx * 2 + part % 2, :, lane : lane + 128] = grad[
                    xx * 64 : xx * 64 + 64, part * 128 : part * 128 + 128
                ]

    def fs_copy(i):
        slot = lax.rem(x + i // 2, 4) * 2 + lax.rem(c + lax.rem(i, 2), 2)
        return pltpu.make_async_remote_copy(
            fs.at[slot], fr.at[i], fr_send, fr_recv,
            device_id=cx_dev(i), device_id_type=MESH,
        )

    def fs_start(i, carry):
        fs_copy(i).start()
        return carry

    lax.fori_loop(1, 8, fs_start, 0)
    fr[pl.ds(0, 1)] = fs[pl.ds(x * 2 + c, 1)]
    take(fr.at[pl.ds(1, 7)], fr_recv)

    def fs_sum(l_to, carry):
        at = pl.ds(pl.multiple_of(l_to * 16, 16), 16)
        total = fr[0, at, :].astype(F32)
        for slot in range(1, 8):
            total = total + fr[slot, at, :].astype(F32)
        total = total.astype(BF16)
        gsend[pl.ds(l_to, 1)] = total[:, :256][None]
        gsend[pl.ds(4 + l_to, 1)] = total[:, 256:][None]
        return carry

    lax.fori_loop(0, 4, fs_sum, 0)

    def gr_copy(d):
        return pltpu.make_async_remote_copy(
            gsend.at[lax.rem(y + d, 8)], grecv.at[d], gr_send, gr_recv,
            device_id=y_dev(d), device_id_type=MESH,
        )

    def gr_start(d, carry):
        gr_copy(d).start()
        return carry

    lax.fori_loop(1, 8, gr_start, 0)
    grecv[pl.ds(0, 1)] = gsend[pl.ds(y, 1)]
    take(grecv.at[pl.ds(1, 7)], gr_recv)
    total = jnp.sum(grecv[...].astype(F32), axis=0)
    for m in range(2):
        gs_ref[m] = (
            total[:, m * 128 : m * 128 + 128] * sfac[m, pl.ds(q, 1)][0, 0:1, :]
        )

    take(pg.at[pl.ds(0, 31)], pg_send)
    take(tx.at[:, pl.ds(0, 3)], tx_send)
    take(sx.at[:, pl.ds(0, 3)], sx_send)
    take(colbuf.at[pl.ds(1, 7)], col_send)
    take(rowbuf1.at[pl.ds(1, 7)], row1_send)
    take(rowbuf2.at[pl.ds(1, 7)], row2_send)
    take(fr.at[pl.ds(1, 7)], fr_send)
    take(grecv.at[pl.ds(1, 7)], gr_send)
    take(rr.at[pl.ds(0, 31)], rr_send)
    take(rr.at[pl.ds(0, 31)], rr_recv)
    for part in range(4):
        total = rr[part].astype(F32)
        for zz in range(1, 8):
            total = total + rr[zz * 4 + part].astype(F32)
        gp_ref[:, part * 1024 : part * 1024 + 512] = total[0:8, :]
        gp_ref[:, part * 1024 + 512 : part * 1024 + 1024] = total[8:16, :]


def local(student_patches, teacher_patches, positions, prototypes, loss_scale):
    vmem = pl.BlockSpec(memory_space=pltpu.VMEM)
    hbm = pl.BlockSpec(memory_space=pltpu.HBM)
    dma = pltpu.SemaphoreType.DMA
    grad_t, grad_protos = pl.pallas_call(
        kernel,
        out_shape=(
            pltpu.VMEM((2, 16, 128), F32),
            pltpu.VMEM((8, 4096), F32),
        ),
        in_specs=[hbm] * 4,
        out_specs=(vmem, vmem),
        scratch_shapes=[
            pltpu.VMEM((2, 2, 256, 256), BF16),
            pltpu.VMEM((2, 2, 256, 256), BF16),
            pltpu.VMEM((2, 2, 64), jnp.int32),
            pltpu.VMEM((8, 4096), BF16),
            pltpu.VMEM((4, 16, 512), BF16),
            pltpu.VMEM((32, 16, 512), BF16),
            pltpu.VMEM((256, 1024), F32),
            pltpu.VMEM((256, 1024), BF16),
            pltpu.VMEM((8, 1024), F32),
            pltpu.VMEM((2, 4, 128, 256), BF16),
            pltpu.VMEM((2, 4, 128, 256), BF16),
            pltpu.VMEM((2, 512, 256), BF16),
            pltpu.VMEM((2, 512, 256), BF16),
            pltpu.VMEM((2, 256, 512), BF16),
            pltpu.VMEM((2, 256, 512), F32),
            pltpu.VMEM((2, 4, 8, 128), F32),
            pltpu.VMEM((2, 512, 1024), F32),
            pltpu.VMEM((2, 512, 1024), F32),
            pltpu.VMEM((2, 512, 1024), BF16),
            pltpu.VMEM((8, ITERS, 2, 8, 128), F32),
            pltpu.VMEM((8, ITERS, 2, 8, 128), F32),
            pltpu.VMEM((8, ITERS, 2, 8, 128), F32),
            pltpu.VMEM((2, 8, 128), F32),
            pltpu.VMEM((2, 512, 128), F32),
            pltpu.VMEM((2, 512, 128), F32),
            pltpu.VMEM((32, 16, 512), BF16),
            pltpu.VMEM((32, 16, 512), BF16),
            pltpu.VMEM((256, 1024), F32),
            pltpu.VMEM((8, 64, 512), BF16),
            pltpu.VMEM((8, 64, 512), BF16),
            pltpu.VMEM((8, 16, 256), BF16),
            pltpu.VMEM((8, 16, 256), BF16),
            dma((4,)),
            dma(()),
            dma((4,)),
            dma((2,)),
            dma(()),
            dma((3,)),
            dma(()),
            dma((3,)),
            dma(()),
            dma((ITERS, 2)),
            dma(()),
            dma((ITERS, 2)),
            dma(()),
            dma((ITERS, 2)),
            dma(()),
            dma(()),
            dma(()),
            dma(()),
            dma(()),
            dma(()),
        ],
        compiler_params=pltpu.CompilerParams(
            collective_id=0, has_side_effects=True, vmem_limit_bytes=60 * 2**20
        ),
        cost_estimate=pl.CostEstimate(
            flops=2_200_000_000, bytes_accessed=2_000_000, transcendentals=2_000_000
        ),
        name="ibot_head",
    )(student_patches, teacher_patches, positions, prototypes)
    factor = loss_scale[0] * (1.0 / (2 * 4096 * 0.1))
    return jnp.transpose(grad_t, (0, 2, 1)) * factor, grad_protos * factor


def solution(mesh):
    in_specs = (
        P(None, "rows", None, None),
        P(None, "rows", None, None),
        P(None, "rows", None),
        P("rows", "protos"),
        P(),
    )
    out_specs = (P(None, "rows", "protos"), P("rows", "protos"))
    return jax.shard_map(local, mesh=mesh, in_specs=in_specs, out_specs=out_specs, check_vma=False)
```

```python
import math

import jax
import jax.numpy as jnp
from jax import lax
from jax.experimental import pallas as pl
from jax.experimental.pallas import tpu as pltpu
from jax.sharding import PartitionSpec as P

ITERS = 3
LOG2E = 1.4426950408889634
TEACHER_EXP2 = LOG2E / 0.07
STUDENT_EXP2 = LOG2E / 0.1
EPSILON = 1e-6
MESH = pl.DeviceIdType.MESH
F32 = jnp.float32
BF16 = jnp.bfloat16


def dot(a, b, ca, cb):
    return lax.dot_general(a, b, (((ca,), (cb,)), ((), ())), preferred_element_type=F32)


def kernel(
    sp_hbm, tp_hbm, pos_hbm, pr_hbm,
    gs_ref, gp_ref,
    sp, tp, pos_ref, pr_ref, send_p, pg, pu, ph, pfac,
    tx, sx, th, sh, sht, ut, sfac,
    kmat, emat, slopes,
    colbuf, rowbuf1, rowbuf2, csc, rb, tb,
    send_r, rr, pterm, fs, fr, gsend, grecv,
    local_sem, pg_send, pg_recv, ring_recv,
    tx_send, tx_recv, sx_send, sx_recv,
    col_send, col_recv, row1_send, row1_recv, row2_send, row2_recv,
    rr_send, rr_recv, fr_send, fr_recv, gr_send, gr_recv,
):
    me = lax.axis_index("rows")
    mp = lax.axis_index("protos")
    z, h, c = me // 4, lax.rem(me // 2, 2), lax.rem(me, 2)
    x, l = mp // 4, lax.rem(mp, 4)
    q = h * 2 + c
    y = h * 4 + l

    def take(ref, sem):
        pltpu.make_async_copy(ref, ref, sem).wait()

    def z_dev(d):
        return (lax.rem(z + d, 8) * 4 + q, mp)

    def cx_dev(i):
        dx, dc = i // 2, lax.rem(i, 2)
        return (z * 4 + h * 2 + lax.rem(c + dc, 2), lax.rem(x + dx, 4) * 4 + l)

    def y_dev(d):
        other = lax.rem(y + d, 8)
        return (z * 4 + (other // 4) * 2 + c, x * 4 + lax.rem(other, 4))

    core_dev = (z * 4 + h * 2 + (1 - c), mp)
    y4_dev = (z * 4 + (1 - h) * 2 + c, mp)
    diag_dev = (z * 4 + (1 - h) * 2 + (1 - c), mp)

    barrier = pltpu.get_barrier_semaphore()
    pl.semaphore_signal(barrier, inc=1, device_id=diag_dev, device_id_type=MESH)

    def greet(d, carry):
        for group in (z_dev, y_dev, cx_dev):
            pl.semaphore_signal(barrier, inc=1, device_id=group(d), device_id_type=MESH)
        return carry

    lax.fori_loop(1, 8, greet, 0)

    load_p = pltpu.make_async_copy(pr_hbm, pr_ref, local_sem.at[2])
    load_p.start()
    load_pos = pltpu.make_async_copy(pos_hbm, pos_ref, local_sem.at[3])
    load_pos.start()
    load_t = pltpu.make_async_copy(tp_hbm, tp, local_sem.at[0])
    load_t.start()
    load_s = pltpu.make_async_copy(sp_hbm, sp, local_sem.at[1])
    load_s.start()

    load_p.wait()
    wide = pr_ref[...].astype(F32)
    for other in range(4):
        first = wide[:, other * 1024 : other * 1024 + 512]
        second = wide[:, other * 1024 + 512 : other * 1024 + 1024]
        send_p[other] = jnp.concatenate([first, second], axis=0).astype(BF16)
    pg[pl.ds(me, 1)] = send_p[pl.ds(q, 1)]

    pl.semaphore_wait(barrier, 22)

    def relative(j):
        return (h + (j // 2)) % 2 * 2 + (c + j % 2) % 2

    def quad_copy(j, target):
        return pltpu.make_async_remote_copy(
            send_p.at[relative(j)], pg.at[me], pg_send, pg_recv.at[j],
            device_id=target, device_id_type=MESH,
        )

    quad_copies = [quad_copy(2, y4_dev), quad_copy(3, diag_dev), quad_copy(1, core_dev)]

    def ring_copy(j, d):
        at = z * 4 + relative(j)
        return pltpu.make_async_remote_copy(
            pg.at[at], pg.at[at], pg_send, ring_recv.at[j // 2],
            device_id=z_dev(d), device_id_type=MESH,
        )

    def ring_start(j):
        for d in (4, 5, 3, 6, 2, 7, 1):
            ring_copy(j, d).start()

    for copy in quad_copies:
        copy.start()
    ring_start(0)
    quad_copies[2].wait_recv()
    ring_start(1)

    def pick(patches, m):
        parts = []
        for image in range(2):
            where = jnp.broadcast_to(pos_ref[m, image : image + 1, :], (256, 64))
            hot = (lax.broadcasted_iota(jnp.int32, (256, 64), 0) == where).astype(F32).astype(BF16)
            parts.append(dot(hot, patches[m, image], 0, 0))
        return jnp.concatenate(parts, axis=0).astype(BF16)

    q_far = (1 - h) * 2 + c
    mine = pl.ds(pl.multiple_of(x * 32, 32), 32)

    def far_copy(buf, send, recv, i):
        return pltpu.make_async_remote_copy(
            buf.at[:, q_far, mine], buf.at[:, q_far, mine], send, recv.at[2],
            device_id=cx_dev(i), device_id_type=MESH,
        )

    def y4_copy(buf, send, recv):
        return pltpu.make_async_remote_copy(
            buf.at[:, q, mine], buf.at[:, q, mine], send, recv.at[1],
            device_id=y4_dev, device_id_type=MESH,
        )

    def core_copy(buf, send, recv):
        return pltpu.make_async_remote_copy(
            buf.at[:, q], buf.at[:, q], send, recv.at[0],
            device_id=core_dev, device_id_type=MESH,
        )

    load_pos.wait()
    load_t.wait()
    for m in range(2):
        tx[m, pl.ds(q, 1)] = pick(tp, m)[None]
    y4_copy(tx, tx_send, tx_recv).start()
    core_copy(tx, tx_send, tx_recv).start()
    load_s.wait()
    for m in range(2):
        sx[m, pl.ds(q, 1)] = pick(sp, m)[None]
    y4_copy(sx, sx_send, sx_recv).start()
    core_copy(sx, sx_send, sx_recv).start()

    def forward_far(buf, send, recv):
        y4_copy(buf, send, recv).wait_recv()

        def body(i, carry):
            far_copy(buf, send, recv, i).start()
            return carry

        lax.fori_loop(1, 8, body, 0)

    def rows_arrive(buf, send, recv):
        core_copy(buf, send, recv).wait_recv()
        take(buf.at[:, pl.ds(0, 2), pl.ds(0, 112)], recv.at[2])

    quad_copies[0].wait_recv()
    ring_start(2)
    quad_copies[1].wait_recv()
    ring_start(3)
    forward_far(tx, tx_send, tx_recv)
    forward_far(sx, sx_send, sx_recv)

    rows_arrive(tx, tx_send, tx_recv)
    for m in range(2):
        for part in range(4):
            values = tx[m, part].astype(F32)
            factor = lax.rsqrt(jnp.sum(values * values, axis=1, keepdims=True) + EPSILON)
            th[m, part * 128 : part * 128 + 128, :] = (values * factor).astype(BF16)

    def unpack_half(half):
        def unpack(i, total):
            b = i // 2 * 4 + half * 2 + lax.rem(i, 2)
            block = pg[b].astype(F32)
            rows = jnp.concatenate([block[0:8, :], block[8:16, :]], axis=1)
            pu[pl.ds(pl.multiple_of(b * 8, 8), 8), :] = rows
            return total + rows * rows
        return unpack

    take(pg.at[pl.ds(0, 14)], ring_recv.at[0])
    total = lax.fori_loop(0, 16, unpack_half(h), jnp.zeros((8, 1024), F32))
    take(pg.at[pl.ds(0, 14)], ring_recv.at[1])
    total = lax.fori_loop(0, 16, unpack_half(1 - h), total)
    pfac[...] = jnp.broadcast_to(
        lax.rsqrt(jnp.sum(total, axis=0, keepdims=True) + EPSILON), (8, 1024)
    )

    def normalize(b, carry):
        at = pl.ds(pl.multiple_of(b * 16, 16), 16)
        unit = pu[at, :] * pfac[0:1, :]
        pu[at, :] = unit
        ph[at, :] = unit.astype(BF16)
        return carry

    lax.fori_loop(0, 16, normalize, 0)

    ring_order = (4, 5, 3, 6, 2, 7, 1)
    cx_order = (4, 5, 2, 3, 6, 7, 1)

    def tile_send(buf, it, m, send, recv, group):
        devices, order = group
        for d in order:
            pltpu.make_async_remote_copy(
                buf.at[0, it, m], buf.at[d, it, m], send, recv.at[it, m],
                device_id=devices[d], device_id_type=MESH,
            ).start()

    def tile_recv(buf, it, m, recv):
        take(buf.at[pl.ds(1, 7), it, m], recv.at[it, m])
        return jnp.sum(buf[:, it, m], axis=0)

    z_group = ([z_dev(d) for d in range(8)], ring_order)
    y_group = ([y_dev(d) for d in range(8)], ring_order)
    cx_group = ([cx_dev(d) for d in range(8)], cx_order)

    def col_store(it, m, tile, sums):
        width = sums.shape[1] // 128
        for part in range(width):
            row = tile * width + part
            colbuf[0, it, m, row : row + 1, :] = sums[:, part * 128 : part * 128 + 128]

    def lane_sums(block):
        return jnp.sum(block.T, axis=0, keepdims=True)

    def spread(row):
        return jnp.broadcast_to(row, (128, 128)).T

    def col_send_start(it, m):
        tile_send(colbuf, it, m, col_send, col_recv, z_group)

    for m in range(2):
        for tile in range(4):
            at = slice(tile * 256, tile * 256 + 256)
            scores = dot(th[m], ph[:, at], 1, 0)
            values = jnp.exp2(scores * TEACHER_EXP2)
            kmat[m, :, at] = values
            col_store(0, m, tile, jnp.sum(values, axis=0, keepdims=True))
        col_send_start(0, m)

    rows_arrive(sx, sx_send, sx_recv)
    for m in range(2):
        for part in range(4):
            values = sx[m, part].astype(F32)
            turned = jnp.concatenate([values[:, :128].T, values[:, 128:].T], axis=0)
            factor = lax.rsqrt(jnp.sum(turned * turned, axis=0, keepdims=True) + EPSILON)
            unit = turned * factor
            at = slice(part * 128, part * 128 + 128)
            ut[m, :, at] = unit
            sht[m, :, at] = unit.astype(BF16)
            sfac[m, part] = jnp.broadcast_to(factor, (8, 128))
            sh[m, at, :] = jnp.concatenate([unit[:128, :].T, unit[128:, :].T], axis=1).astype(BF16)

    for m in range(2):
        acc = None
        for tile in range(4):
            at = slice(tile * 256, tile * 256 + 256)
            logits = dot(sh[m], ph[:, at], 1, 0)
            values = jnp.exp2(logits * STUDENT_EXP2)
            emat[m, :, at] = values
            half = values[:, :128] + values[:, 128:]
            acc = half if acc is None else acc + half
        for part in range(4):
            rowbuf1[0, 0, m, 4 + part : 5 + part, :] = lane_sums(acc[part * 128 : part * 128 + 128, :])

    for it in range(ITERS):
        for m in range(2):
            total = tile_recv(colbuf, it, m, col_recv)
            csc[m] = 1.0 / total
            for part in range(4):
                at = slice(part * 128, part * 128 + 128)
                acc = jnp.zeros((128, 128), F32)
                for tile in range(8):
                    acc = acc + kmat[m, at, tile * 128 : tile * 128 + 128] * csc[m, tile : tile + 1, :]
                rowbuf1[0, it, m, part : part + 1, :] = lane_sums(acc)
            if it > 0:
                rowbuf1[0, it, m, 4:8, :] = jnp.zeros((4, 128), F32)
            tile_send(rowbuf1, it, m, row1_send, row1_recv, cx_group)
        if it == 1:
            for m in range(2):
                for tile in range(8):
                    at = slice(tile * 128, tile * 128 + 128)
                    emat[m, :, at] = emat[m, :, at] * tb[m]
        if it == ITERS - 1:
            for m in range(2):
                for tile in range(8):
                    at = slice(tile * 128, tile * 128 + 128)
                    kmat[m, :, at] = kmat[m, :, at] * csc[m, tile : tile + 1, :]
        for m in range(2):
            total = tile_recv(rowbuf1, it, m, row1_recv)
            rowbuf2[0, it, m] = total
            tile_send(rowbuf2, it, m, row2_send, row2_recv, y_group)
        for m in range(2):
            total = tile_recv(rowbuf2, it, m, row2_recv)
            inverse = 1.0 / total[0:4, :]
            for part in range(4):
                rb[m, part * 128 : part * 128 + 128, :] = spread(inverse[part : part + 1, :])
            if it == 0:
                denominator = 1.0 / total[4:8, :]
                for part in range(4):
                    tb[m, part * 128 : part * 128 + 128, :] = spread(denominator[part : part + 1, :])
            if it < ITERS - 1:
                for tile in range(8):
                    at = slice(tile * 128, tile * 128 + 128)
                    sums = jnp.sum(kmat[m, :, at] * rb[m], axis=0, keepdims=True)
                    col_store(it + 1, m, tile, sums)
                col_send_start(it + 1, m)

    for tile in range(4):
        at = slice(tile * 256, tile * 256 + 256)
        proto_sum = None
        for m in range(2):
            scale = jnp.concatenate([rb[m]] * 2, axis=1)
            values = (emat[m, :, at] - kmat[m, :, at] * scale).astype(BF16)
            slopes[m, :, at] = values
            term = dot(sht[m], values, 1, 0)
            proto_sum = term if proto_sum is None else proto_sum + term
        unit = pu[:, at]
        column_dot = jnp.sum(unit * proto_sum, axis=0, keepdims=True)
        pterm[:, at] = (proto_sum - unit * column_dot) * pfac[0:1, at]

    def send_back(d, carry):
        target = lax.rem(me + d, 32)
        rows = pterm[pl.ds(pl.multiple_of(target * 8, 8), 8), :]
        packed = jnp.concatenate([rows[:, :512], rows[:, 512:]], axis=0)
        send_r[pl.ds(d, 1)] = packed.astype(BF16)[None]
        pltpu.make_async_remote_copy(
            send_r.at[d], rr.at[me], rr_send.at[d], rr_recv.at[d],
            device_id=(target, mp), device_id_type=MESH,
        ).start()
        return carry

    def back_to(i):
        step = i // 4
        dz = lax.rem(4 + (step + 1) // 2 * (2 * lax.rem(step, 2) - 1), 8)
        j = 3 - lax.rem(i, 4)
        q_to = lax.rem(h + j // 2, 2) * 2 + lax.rem(c + lax.rem(j, 2), 2)
        return lax.rem(z + dz, 8) * 4 + q_to

    def rr_copy(i):
        return pltpu.make_async_remote_copy(
            send_r.at[i], rr.at[me], rr_send, rr_recv,
            device_id=(back_to(i), mp), device_id_type=MESH,
        )

    def send_back(i, carry):
        rows = pterm[pl.ds(pl.multiple_of(back_to(i) * 8, 8), 8), :]
        packed = jnp.concatenate([rows[:, :512], rows[:, 512:]], axis=0)
        send_r[pl.ds(i, 1)] = packed.astype(BF16)[None]
        rr_copy(i).start()
        return carry

    lax.fori_loop(0, 31, send_back, 0)
    own = pterm[pl.ds(pl.multiple_of(me * 8, 8), 8), :]
    rr[pl.ds(me, 1)] = jnp.concatenate([own[:, :512], own[:, 512:]], axis=0).astype(BF16)[None]

    for m in range(2):
        grad = dot(ph[...], slopes[m], 1, 1)
        unit = ut[m]
        inner = jnp.sum(unit * grad, axis=0, keepdims=True)
        grad = (grad - unit * inner).astype(BF16)
        for xx in range(4):
            for part in range(4):
                lane = ((part // 2) * 2 + m) * 128
                fs[xx * 2 + part % 2, :, lane : lane + 128] = grad[
                    xx * 64 : xx * 64 + 64, part * 128 : part * 128 + 128
                ]

    def fs_copy(i):
        slot = lax.rem(x + i // 2, 4) * 2 + lax.rem(c + lax.rem(i, 2), 2)
        return pltpu.make_async_remote_copy(
            fs.at[slot], fr.at[i], fr_send, fr_recv,
            device_id=cx_dev(i), device_id_type=MESH,
        )

    def fs_start(i, carry):
        fs_copy(i).start()
        return carry

    lax.fori_loop(1, 8, fs_start, 0)
    fr[pl.ds(0, 1)] = fs[pl.ds(x * 2 + c, 1)]
    take(fr.at[pl.ds(1, 7)], fr_recv)

    def fs_sum(l_to, carry):
        at = pl.ds(pl.multiple_of(l_to * 16, 16), 16)
        total = fr[0, at, :].astype(F32)
        for slot in range(1, 8):
            total = total + fr[slot, at, :].astype(F32)
        total = total.astype(BF16)
        gsend[pl.ds(l_to, 1)] = total[:, :256][None]
        gsend[pl.ds(4 + l_to, 1)] = total[:, 256:][None]
        return carry

    lax.fori_loop(0, 4, fs_sum, 0)

    def gr_copy(d):
        return pltpu.make_async_remote_copy(
            gsend.at[lax.rem(y + d, 8)], grecv.at[d], gr_send, gr_recv,
            device_id=y_dev(d), device_id_type=MESH,
        )

    def gr_start(d, carry):
        gr_copy(d).start()
        return carry

    lax.fori_loop(1, 8, gr_start, 0)
    grecv[pl.ds(0, 1)] = gsend[pl.ds(y, 1)]
    take(grecv.at[pl.ds(1, 7)], gr_recv)
    total = jnp.sum(grecv[...].astype(F32), axis=0)
    for m in range(2):
        gs_ref[m] = (
            total[:, m * 128 : m * 128 + 128] * sfac[m, pl.ds(q, 1)][0, 0:1, :]
        )

    take(pg.at[pl.ds(0, 31)], pg_send)
    take(tx.at[:, pl.ds(0, 3)], tx_send)
    take(sx.at[:, pl.ds(0, 3)], sx_send)
    take(colbuf.at[pl.ds(1, 7)], col_send)
    take(rowbuf1.at[pl.ds(1, 7)], row1_send)
    take(rowbuf2.at[pl.ds(1, 7)], row2_send)
    take(fr.at[pl.ds(1, 7)], fr_send)
    take(grecv.at[pl.ds(1, 7)], gr_send)
    take(rr.at[pl.ds(0, 31)], rr_send)
    take(rr.at[pl.ds(0, 31)], rr_recv)
    for part in range(4):
        total = rr[part].astype(F32)
        for zz in range(1, 8):
            total = total + rr[zz * 4 + part].astype(F32)
        gp_ref[:, part * 1024 : part * 1024 + 512] = total[0:8, :]
        gp_ref[:, part * 1024 + 512 : part * 1024 + 1024] = total[8:16, :]


def local(student_patches, teacher_patches, positions, prototypes, loss_scale):
    vmem = pl.BlockSpec(memory_space=pltpu.VMEM)
    hbm = pl.BlockSpec(memory_space=pltpu.HBM)
    dma = pltpu.SemaphoreType.DMA
    grad_t, grad_protos = pl.pallas_call(
        kernel,
        out_shape=(
            pltpu.VMEM((2, 16, 128), F32),
            pltpu.VMEM((8, 4096), F32),
        ),
        in_specs=[hbm] * 4,
        out_specs=(vmem, vmem),
        scratch_shapes=[
            pltpu.VMEM((2, 2, 256, 256), BF16),
            pltpu.VMEM((2, 2, 256, 256), BF16),
            pltpu.VMEM((2, 2, 64), jnp.int32),
            pltpu.VMEM((8, 4096), BF16),
            pltpu.VMEM((4, 16, 512), BF16),
            pltpu.VMEM((32, 16, 512), BF16),
            pltpu.VMEM((256, 1024), F32),
            pltpu.VMEM((256, 1024), BF16),
            pltpu.VMEM((8, 1024), F32),
            pltpu.VMEM((2, 4, 128, 256), BF16),
            pltpu.VMEM((2, 4, 128, 256), BF16),
            pltpu.VMEM((2, 512, 256), BF16),
            pltpu.VMEM((2, 512, 256), BF16),
            pltpu.VMEM((2, 256, 512), BF16),
            pltpu.VMEM((2, 256, 512), F32),
            pltpu.VMEM((2, 4, 8, 128), F32),
            pltpu.VMEM((2, 512, 1024), F32),
            pltpu.VMEM((2, 512, 1024), F32),
            pltpu.VMEM((2, 512, 1024), BF16),
            pltpu.VMEM((8, ITERS, 2, 8, 128), F32),
            pltpu.VMEM((8, ITERS, 2, 8, 128), F32),
            pltpu.VMEM((8, ITERS, 2, 8, 128), F32),
            pltpu.VMEM((2, 8, 128), F32),
            pltpu.VMEM((2, 512, 128), F32),
            pltpu.VMEM((2, 512, 128), F32),
            pltpu.VMEM((32, 16, 512), BF16),
            pltpu.VMEM((32, 16, 512), BF16),
            pltpu.VMEM((256, 1024), F32),
            pltpu.VMEM((8, 64, 512), BF16),
            pltpu.VMEM((8, 64, 512), BF16),
            pltpu.VMEM((8, 16, 256), BF16),
            pltpu.VMEM((8, 16, 256), BF16),
            dma((4,)),
            dma(()),
            dma((4,)),
            dma((2,)),
            dma(()),
            dma((3,)),
            dma(()),
            dma((3,)),
            dma(()),
            dma((ITERS, 2)),
            dma(()),
            dma((ITERS, 2)),
            dma(()),
            dma((ITERS, 2)),
            dma(()),
            dma(()),
            dma(()),
            dma(()),
            dma(()),
            dma(()),
        ],
        compiler_params=pltpu.CompilerParams(
            collective_id=0, has_side_effects=True, vmem_limit_bytes=60 * 2**20
        ),
        cost_estimate=pl.CostEstimate(
            flops=2_200_000_000, bytes_accessed=2_000_000, transcendentals=2_000_000
        ),
        name="ibot_head",
    )(student_patches, teacher_patches, positions, prototypes)
    factor = loss_scale[0] * (1.0 / (2 * 4096 * 0.1))
    return jnp.transpose(grad_t, (0, 2, 1)) * factor, grad_protos * factor


def solution(mesh):
    in_specs = (
        P(None, "rows", None, None),
        P(None, "rows", None, None),
        P(None, "rows", None),
        P("rows", "protos"),
        P(),
    )
    out_specs = (P(None, "rows", "protos"), P("rows", "protos"))
    return jax.shard_map(local, mesh=mesh, in_specs=in_specs, out_specs=out_specs, check_vma=False)
```
